256 devices in a mesh: rows: 64 (over x, z, core), scales: 4 (over y).
Axes of the slice: x: 4, y: 4, z: 8, core: 2. Of those that a mesh axis runs over, the one named last changes fastest.
Arguments:
- image_now: float32 [2048, 8192], P(('rows', 'scales')), may hold values from 0.1 to 4
- gradient: float32 [2048, 8192], P(('rows', 'scales')), may hold values from -140 to 140
- hessian_weight: float32 [2048, 8192], P(('rows', 'scales')), may hold values from 0.1 to 10
- psf_tiles: float32 [256, 256], P(('rows', 'scales')), may hold values from -0.5 to 1.7
- facet_of_row: int32 [2048], P(('rows', 'scales')), may hold values from 0 to 255, never falling along the last dimension, each value on 1 to 32 neighbouring positions
- tile_slot: int32 [256], replicated, may hold values from 0 to 255, each once
- thresholds: float32 [4], replicated, may hold values from 0.2 to 2
Outputs:
- new_image: float32 [2048, 8192], P(('rows', 'scales'))
The draws below stay inside these ranges and needn't reach their ends.
Inputs may be any that keep to these rules, and one draw needn't show every extreme that they name: `facet_of_row`: facet numbers never fall along the rows; every facet covers 1 to 32 rows, and some facet exactly 32. `tile_slot`: each facet's tile stands in a different row of psf_tiles, and every row holds one.
All inputs are finite; a program needn't handle non-finite values.
Results may differ from the reference program's by a relative error of at most 0.0001.
Values sent between devices are 32-bit elements; how exact they have to be, the bound alone decides.
No kernel may reach another device: no remote copies, remote signals or barrier semaphores. Data moves between devices by JAX's collectives and lax.ppermute only.
A program may use at most 64 MiB of HBM per device.

```python
import math
import jax
import jax.numpy as jnp
import numpy as np
from jax import lax

COLS = 8192
TILE = 16
SUBITERS = 2
SCALES = 4
HEIGHT = 2048
FACETS = 256
FMOST = 32


def draw_gradient(key, part):
    key_noise, key_rows, key_cols = jax.random.split(key, 3)
    position = jnp.arange(HEIGHT, dtype=jnp.float32)[:, None] / HEIGHT
    rising = jnp.exp(math.log(3.0) * position)
    row_scale = jnp.exp(jax.random.uniform(key_rows, (HEIGHT, 1), minval=0.0, maxval=math.log(10.0))) * rising
    col_scale = jnp.exp(jax.random.uniform(key_cols, (1, COLS), minval=0.0, maxval=math.log(10.0)))
    pattern = jnp.clip(jax.random.normal(key_noise, (HEIGHT, COLS)), -6.0, 6.0)
    return (0.03 * pattern * row_scale * col_scale).astype(jnp.float32)


def draw_hessian_weight(key, part):
    key_cells, key_rows = jax.random.split(key, 2)
    cells = jnp.exp(jax.random.uniform(key_cells, (HEIGHT, COLS), minval=math.log(0.1), maxval=0.0))
    row_scale = jnp.exp(jax.random.uniform(key_rows, (HEIGHT, 1), minval=0.0, maxval=math.log(10.0)))
    return (cells * row_scale).astype(jnp.float32)


def draw_psf_tiles(key, part):
    key_side, key_peak = jax.random.split(key, 2)
    centre = (jnp.arange(TILE * TILE) == TILE // 2 * TILE + TILE // 2)[None, :]
    side_lobes = 0.1 * jnp.clip(jax.random.normal(key_side, (FACETS, TILE * TILE)), -4.0, 4.0)
    peak_value = jax.random.uniform(key_peak, (FACETS, 1), minval=0.8, maxval=1.2)
    return jnp.where(centre, peak_value + side_lobes, side_lobes).astype(jnp.float32)


def level_of(key, shape, cuts, least, largest):
    def one(dim, parts):
        heights = jax.random.uniform(jax.random.fold_in(jax.random.fold_in(key, 6), dim), (parts,), jnp.float32, least / len(cuts), largest / len(cuts))
        return jnp.repeat(jnp.exp(heights), shape[dim] // parts).reshape((-1,) + (1,) * (len(shape) - dim - 1))

    gain = one(*cuts[0])
    for cut in cuts[1:]:
        gain = gain * one(*cut)
    return gain


def profile(number_of, total, reach, slope):
    loads = [(1 << 20) // math.isqrt(grade ** slope) + 1 for grade in range(2, number_of + 1)]
    spare, given = total - reach - (number_of - 1), [1] * (number_of - 1)
    while spare > 0:
        movable = [i for i in range(number_of - 1) if given[i] < reach]
        whole, budget = sum([loads[i] for i in movable]), spare
        for i in movable:
            extra = min(reach - given[i], max(1, budget * loads[i] // whole), spare)
            given[i] = given[i] + extra
            spare = spare - extra
    return np.array([reach] + given)


def ragged_sizes(key, count, total, bound, lean):
    if count == 2:
        one = jax.random.randint(key, (), max(1, total - bound), min(bound, total - 1) + 1)
        return jnp.stack([one, total - one])
    sizes = jnp.asarray(profile(count, total, bound, lean), jnp.int32)
    couples = (count - 1) // 2
    source_of, receiver = sizes[1:1 + 2 * couples:2], sizes[2:2 + 2 * couples:2]
    slack = jnp.minimum(source_of - 1, bound - receiver)
    moved = jax.random.randint(jax.random.fold_in(key, 1), (couples,), 0, 1 << 20) % (slack + 1)
    sizes = sizes.at[1:1 + 2 * couples:2].set(source_of - moved).at[2:2 + 2 * couples:2].set(receiver + moved)
    return sizes[jax.random.permutation(jax.random.fold_in(key, 2), count)]


def setup_inputs(seed: int = 0) -> dict:
    streams_of = jax.random.split(jax.random.key(seed), 8)
    return {
        "image_now": jnp.clip(jnp.exp(math.log(4.0) - 3.6888794 * jax.random.uniform(streams_of[0], (HEIGHT, COLS), jnp.float32) ** level_of(streams_of[0], (HEIGHT, COLS), ((0, 256),), -0.2, 0.2)), 0.1, 4.0),
        "gradient": draw_gradient(jax.random.fold_in(streams_of[7], 71), 0),
        "hessian_weight": draw_hessian_weight(jax.random.fold_in(streams_of[7], 71), 0),
        "psf_tiles": draw_psf_tiles(jax.random.fold_in(streams_of[7], 71), 0),
        "facet_of_row": jnp.searchsorted(jnp.cumsum(ragged_sizes(streams_of[4], FACETS, HEIGHT, FMOST, 2)), jnp.arange(HEIGHT), side="right").astype(jnp.int32),
        "tile_slot": jax.random.permutation(streams_of[5], FACETS).astype(jnp.int32),
        "thresholds": jnp.clip(jnp.exp(jax.random.uniform(streams_of[6], (SCALES,), jnp.float32, math.log(0.2), math.log(2.0))), 0.2, 2.0),
    }


SPLINE_EDGE = 0.0625
SPLINE_NEAR = 0.25
SPLINE_MID = 0.375


def along_columns(source, spacing):
    length = source.shape[1]
    padded = jnp.pad(source, ((0, 0), (2 * spacing, 2 * spacing)))
    outer_pair = padded[:, 0:length] + padded[:, 4 * spacing:4 * spacing + length]
    inner_pair = padded[:, spacing:spacing + length] + padded[:, 3 * spacing:3 * spacing + length]
    return SPLINE_EDGE * outer_pair + SPLINE_NEAR * inner_pair + SPLINE_MID * source


def along_rows(source, spacing):
    length = source.shape[0]
    padded = jnp.pad(source, ((2 * spacing, 2 * spacing), (0, 0)))
    outer_pair = padded[0:length] + padded[4 * spacing:4 * spacing + length]
    inner_pair = padded[spacing:spacing + length] + padded[3 * spacing:3 * spacing + length]
    return SPLINE_EDGE * outer_pair + SPLINE_NEAR * inner_pair + SPLINE_MID * source


def forward_blur(source, weights):
    height, columns = source.shape
    half_tile = TILE // 2
    padded = jnp.pad(source, ((half_tile, half_tile), (half_tile, half_tile)))

    def add_tap_row(tap_row, summed):
        shifted = lax.dynamic_slice_in_dim(padded, tap_row, height, 0)
        tap_weights = lax.dynamic_index_in_dim(weights, tap_row, 1, keepdims=False)
        for column in range(TILE):
            summed = summed + tap_weights[:, column:column + 1] * shifted[:, column:column + columns]
        return summed

    return lax.fori_loop(0, TILE, add_tap_row, jnp.zeros((height, columns), jnp.float32))


def adjoint_blur(source, weights):
    height, columns = source.shape
    half_tile = TILE // 2
    padded = jnp.pad(source, ((half_tile, half_tile), (half_tile, half_tile)))
    wide_weights = jnp.pad(weights, ((half_tile, half_tile), (0, 0), (0, 0)))

    def add_tap_row(tap_row, summed):
        offset = 2 * half_tile - tap_row
        shifted = lax.dynamic_slice_in_dim(padded, offset, height, 0)
        weight_rows = lax.dynamic_slice_in_dim(wide_weights, offset, height, 0)
        tap_weights = lax.dynamic_index_in_dim(weight_rows, tap_row, 1, keepdims=False)
        for column in range(TILE):
            offset_col = 2 * half_tile - column
            summed = summed + tap_weights[:, column:column + 1] * shifted[:, offset_col:offset_col + columns]
        return summed

    return lax.fori_loop(0, TILE, add_tap_row, jnp.zeros((height, columns), jnp.float32))


def shrink(trial, step_size, thresholds):
    smooth = trial
    summed = jnp.zeros_like(trial)
    for depth in range(SCALES):
        smoother = along_rows(along_columns(smooth, 2 ** depth), 2 ** depth)
        detail = smooth - smoother
        limit = step_size * thresholds[depth]
        summed = summed + (detail - jnp.clip(detail, -limit, limit))
        smooth = smoother
    return summed + smooth


def reference(image_now, gradient, hessian_weight, psf_tiles, facet_of_row, tile_slot, thresholds):
    slot_rows = jnp.take(tile_slot, facet_of_row).astype(jnp.int32)
    weights = jnp.take(psf_tiles, slot_rows, axis=0).reshape(HEIGHT, TILE, TILE)
    current = image_now
    for sweep in range(SUBITERS):
        change = current - image_now
        pushed = hessian_weight * forward_blur(change, weights)
        descent = gradient + adjoint_blur(pushed, weights)
        blurred = forward_blur(descent, weights)
        step_size = jnp.sum(descent * descent) / jnp.sum(hessian_weight * blurred * blurred)
        current = shrink(current - step_size * descent, step_size, thresholds)
    return current
```

```python
import functools
import jax
import jax.numpy as jnp
from jax import lax
from jax.experimental import pallas as pl
from jax.experimental.pallas import tpu as pltpu
from jax.sharding import Mesh, PartitionSpec as P

TILE = 16
HALF = TILE // 2
LEVELS = 4
GROUP = 16
SPLIT = 8
BAND = GROUP * SPLIT
WIDE = 512
SIDE = 128
FRAME = WIDE + 2 * SIDE
DEEP = 80
NEAR = 48
MIDDLE = 32
GUARD = 16
F32 = jnp.float32
BF16 = jnp.bfloat16

GROUP_AXES = ("zl", "core", "y")
BAND_AXES = ("x", "zh")
ALL_AXES = ("x", "zh", "zl", "core", "y")

G0, I0, H0, A0, T0 = 0, FRAME, 2 * FRAME, 3 * FRAME, 3 * FRAME + 128
LANES = T0 + 128


def params():
    return pltpu.CompilerParams(vmem_limit_bytes=56 * 1024 * 1024)


def vmem(count):
    return [pl.BlockSpec(memory_space=pltpu.VMEM)] * count


def smem():
    return pl.BlockSpec(memory_space=pltpu.SMEM)


def pack_kernel(grad, image, weight, tile, facet, out):
    columns = grad.shape[1]
    for start, source in ((G0, grad), (I0, image), (H0, weight)):
        for block in range(GROUP):
            low, high = block * WIDE - SIDE, block * WIDE + WIDE + SIDE
            left, right = max(0, -low), max(0, high - columns)
            if left:
                out[block, :, start : start + left] = jnp.zeros((SPLIT, left), F32)
            if right:
                out[block, :, start + FRAME - right : start + FRAME] = jnp.zeros((SPLIT, right), F32)
            out[block, :, start + left : start + FRAME - right] = source[:, low + left : high - right]
    ids = jnp.broadcast_to(facet[...].astype(F32) + 1.0, (SPLIT, 128))
    halves = jnp.concatenate(
        [tile[:, 0:128], tile[:, 128:256], jnp.zeros((SPLIT - 2, 128), F32)], axis=0
    )
    for block in range(GROUP):
        out[block, :, A0 : A0 + 128] = ids
        out[block, :, T0 : T0 + 128] = halves


def split(value):
    high = value.astype(BF16)
    low = (value - high.astype(F32)).astype(BF16)
    return high, low


def iota(shape, dim):
    return lax.broadcasted_iota(jnp.int32, shape, dim)


def dot(a, b):
    return jnp.dot(a, b, preferred_element_type=F32)


def skewed_taps(ids, tiles, slots):
    rows = ids.shape[0]
    facet = jnp.concatenate([ids, ids], axis=1)
    lane = iota((rows, 256), 1).astype(F32) + 1.0
    slot = jnp.sum(jnp.where(facet == lane, slots, 0.0), axis=1, keepdims=True)
    pick = (slot == lane).astype(F32).astype(BF16)
    row, col = iota((256, 256), 0), iota((256, 256), 1)
    order = (row == (col % 16) * 16 + col // 16).astype(F32).astype(BF16)
    turned = (row == (15 - col % 16) * 16 + col // 16).astype(F32).astype(BF16)
    high, low = split(tiles)

    def taps(matrix):
        return dot(pick, dot(high, matrix).astype(BF16)) + dot(pick, dot(low, matrix).astype(BF16))

    forward, backward = taps(order), taps(turned)
    kept = BAND + 2 * MIDDLE
    group = iota((kept, 256), 1) % 16
    adjoint = jnp.zeros((kept, 256), F32)
    for step in range(TILE):
        adjoint = jnp.where(group == step, backward[9 + step : 9 + step + kept], adjoint)
    return (
        pltpu.roll(forward, 0, 1, stride=1, stride_axis=0),
        pltpu.roll(adjoint, 9, 1, stride=1, stride_axis=0),
    )


def banded(skew, first, out, offset):
    rows = skew.shape[0]
    place = iota((rows, 256), 1) - iota((rows, 256), 0) - first - offset
    band = (place >= 0) & (place < TILE)
    for column in range(TILE):
        shift = (256 - 16 * column) % 256
        matrix = jnp.where(band, pltpu.roll(skew, shift, 1) if shift else skew, 0.0)
        high, low = split(matrix)
        out[column, 0:rows, 0:256] = high
        out[column, 0:rows, 256:512] = high
        out[column, 0:rows, 512:768] = low


def load_operand(ref, first, rows, pieces):
    high, low = split(ref[first : first + rows, :])
    for start, part in ((0, high), (256, low), (512, high)):
        pieces[start : start + rows, :] = part
        if rows < 256:
            pieces[start + rows : start + 256, :] = jnp.zeros((256 - rows, FRAME), BF16)


def products(matrix, pieces, rows, planes, chunk):
    for column in range(0, TILE, chunk):
        left = matrix[column : column + chunk, 0:rows, :].reshape(chunk * rows, 768)
        planes[column * rows : (column + chunk) * rows, :] = dot(left, pieces[...])


def shifted_sum(planes, rows, start, size, ahead):
    parts = [planes[pl.ds(b * rows + start, size), :] for b in range(TILE)]
    step = 1
    while len(parts) > 1:
        shift = FRAME - step if ahead else step
        parts = [parts[i] + pltpu.roll(parts[i + 1], shift, 1) for i in range(0, len(parts), 2)]
        step *= 2
    return pltpu.roll(parts[0], HALF if ahead else FRAME - HALF, 1)


def inside(first, rows, band, block):
    row = iota((rows, FRAME), 0) + (first + band * BAND)
    col = iota((rows, FRAME), 1) + (block * WIDE - SIDE)
    return (row >= 0) & (row < BAND * 16) & (col >= 0) & (col < WIDE * GROUP)


def starlet(planes, total, rows, top, limits, band, block):
    size = 16

    def level(depth, last):
        source, target = planes[depth % 2], planes[1 - depth % 2]
        d = 2**depth
        limit = limits[depth]

        def chunk(index, carry):
            start = pl.multiple_of(index * size, size)
            wide = source[pl.ds(start, size + 2 * GUARD), :]

            def rows_at(offset):
                return wide[GUARD + offset : GUARD + offset + size]

            plain = rows_at(0)
            down = 0.0625 * (rows_at(-2 * d) + rows_at(2 * d)) + 0.25 * (rows_at(-d) + rows_at(d)) + 0.375 * plain
            smoother = (
                0.0625 * (pltpu.roll(down, 2 * d, 1) + pltpu.roll(down, FRAME - 2 * d, 1))
                + 0.25 * (pltpu.roll(down, d, 1) + pltpu.roll(down, FRAME - d, 1))
                + 0.375 * down
            )
            smoother = jnp.where(inside(top + start, size, band, block), smoother, 0.0)
            detail = plain - smoother
            kept = detail - jnp.clip(detail, -limit, limit)
            if last:
                kept = kept + smoother
            else:
                target[pl.ds(start + GUARD, size), :] = smoother
            if depth:
                kept = kept + total[pl.ds(start, size), :]
            total[pl.ds(start, size), :] = kept
            return carry

        lax.fori_loop(0, rows // size, chunk, 0)

    for depth in range(LEVELS):
        level(depth, depth == LEVELS - 1)


def clear_guards(plane, rows):
    plane[0:GUARD, :] = jnp.zeros((GUARD, FRAME), F32)
    plane[GUARD + rows : 2 * GUARD + rows, :] = jnp.zeros((GUARD, FRAME), F32)


def put_partials(out, numerator, denominator):
    lane = iota((256, 128), 1)
    out[...] = jnp.where(lane == 0, numerator, jnp.where(lane == 1, denominator, 0.0))


def step_of(sums):
    total = jnp.sum(sums[...], axis=0, keepdims=True)
    lane = iota((1, 128), 1)
    return jnp.sum(jnp.where(lane == 0, total, 0.0)) / jnp.sum(jnp.where(lane == 1, total, 0.0))


def first_kernel(block, grad_up, grad_down, near_up, near_down, tiles, slots, partial, forward, adjoint, frame, matrix, pieces, planes):
    ids = jnp.concatenate(
        [near_up[:, FRAME:], block[:, A0 : A0 + 128], near_down[:, FRAME:]], axis=0
    )
    table = jnp.concatenate(
        [jnp.concatenate([tiles[g, half] for g in range(16)], axis=0) for half in range(2)], axis=1
    )
    ahead, back = skewed_taps(ids, table, slots[...].astype(F32) + 1.0)
    forward[...] = ahead
    adjoint[...] = back
    banded(ahead[NEAR : NEAR + BAND], NEAR, matrix, 0)
    frame[0:DEEP, :] = grad_up[...]
    frame[DEEP : DEEP + BAND, :] = block[:, G0 : G0 + FRAME]
    frame[DEEP + BAND : 2 * DEEP + BAND, :] = grad_down[...]
    load_operand(frame, DEEP - NEAR - HALF, 256, pieces)
    products(matrix, pieces, BAND, planes, 4)
    size = 16

    def chunk(index, carry):
        start = pl.multiple_of(index * size, size)
        blurred = shifted_sum(planes, BAND, start, size, True)[:, SIDE : SIDE + WIDE]
        weight = block[pl.ds(start, size), H0 + SIDE : H0 + SIDE + WIDE]
        grad = block[pl.ds(start, size), G0 + SIDE : G0 + SIDE + WIDE]
        return carry[0] + grad * grad, carry[1] + weight * blurred * blurred

    zero = jnp.zeros((size, WIDE), F32)
    top, bottom = lax.fori_loop(0, BAND // size, chunk, (zero, zero))
    put_partials(partial, jnp.sum(top), jnp.sum(bottom))


def middle_kernel(
    place, thresholds, block, grad_up, grad_down, image_up, image_down, near_up, near_down, sums, forward, adjoint,
    partial, trial,
    grad, image, weight, plane_a, plane_b, total, matrix, pieces, planes, pushed,
):
    band, col = place[0], place[1]
    step = step_of(sums)
    rows = BAND + 2 * DEEP
    near = BAND + 2 * NEAR
    kept = BAND + 2 * MIDDLE
    size = 16
    grad[0:DEEP, :] = grad_up[...]
    grad[DEEP : DEEP + BAND, :] = block[:, G0 : G0 + FRAME]
    grad[DEEP + BAND : rows, :] = grad_down[...]
    image[0:DEEP, :] = image_up[...]
    image[DEEP : DEEP + BAND, :] = block[:, I0 : I0 + FRAME]
    image[DEEP + BAND : rows, :] = image_down[...]
    weight[0:NEAR, :] = near_up[:, 0:FRAME]
    weight[NEAR : NEAR + BAND, :] = block[:, H0 : H0 + FRAME]
    weight[NEAR + BAND : near, :] = near_down[:, 0:FRAME]
    clear_guards(plane_a, rows)
    clear_guards(plane_b, rows)
    plane_a[GUARD : GUARD + rows, :] = image[...] - step * grad[...]
    limits = [step * thresholds[k] for k in range(LEVELS)]
    starlet((plane_a, plane_b), total, rows, -DEEP, limits, band, col)

    first = DEEP - NEAR - HALF
    plane_a[0:256, :] = total[first : first + 256, :] - image[first : first + 256, :]
    load_operand(plane_a, 0, 256, pieces)
    banded(forward[...], 0, matrix, 0)
    products(matrix, pieces, near, planes, 4)

    def push(index, carry):
        start = pl.multiple_of(index * size, size)
        pushed[pl.ds(start, size), :] = weight[pl.ds(start, size), :] * shifted_sum(planes, near, start, size, True)
        return carry

    lax.fori_loop(0, near // size, push, 0)

    load_operand(pushed, 0, near, pieces)
    first = DEEP - MIDDLE
    descent = plane_b
    banded(adjoint[...], 0, matrix, 9)
    products(matrix, pieces, kept, planes, 4)
    descent[0:32, :] = jnp.zeros((32, FRAME), F32)
    descent[24 + kept : 256, :] = jnp.zeros((256 - 24 - kept, FRAME), F32)

    def descend(index, carry):
        start = pl.multiple_of(index * size, size)
        value = grad[pl.ds(start + first, size), :] + shifted_sum(planes, kept, start, size, False)
        value = jnp.where(inside(start - MIDDLE, size, band, col), value, 0.0)
        descent[pl.ds(start + 24, size), :] = value
        trial[0, pl.ds(start, size), :] = total[pl.ds(start + first, size), :]
        trial[1, pl.ds(start, size), :] = value
        return carry

    lax.fori_loop(0, kept // size, descend, 0)

    load_operand(descent, 0, 256, pieces)
    banded(forward[NEAR : NEAR + BAND, :], NEAR, matrix, 0)
    products(matrix, pieces, BAND, planes, 4)

    def chunk(index, carry):
        start = pl.multiple_of(index * size, size)
        blurred = shifted_sum(planes, BAND, start, size, True)[:, SIDE : SIDE + WIDE]
        value = descent[pl.ds(start + 24 + MIDDLE, size), SIDE : SIDE + WIDE]
        heavy = weight[pl.ds(start + NEAR, size), SIDE : SIDE + WIDE]
        return carry[0] + value * value, carry[1] + heavy * blurred * blurred

    zero = jnp.zeros((size, WIDE), F32)
    top, bottom = lax.fori_loop(0, BAND // size, chunk, (zero, zero))
    put_partials(partial, jnp.sum(top), jnp.sum(bottom))


def last_kernel(place, thresholds, trial, sums, out, plane_a, plane_b, total):
    step = step_of(sums)
    rows = BAND + 2 * MIDDLE
    clear_guards(plane_a, rows)
    clear_guards(plane_b, rows)
    plane_a[GUARD : GUARD + rows, :] = trial[0] - step * trial[1]
    limits = [step * thresholds[k] for k in range(LEVELS)]
    starlet((plane_a, plane_b), total, rows, -MIDDLE, limits, place[0], place[1])
    out[...] = total[MIDDLE : MIDDLE + BAND, SIDE : SIDE + WIDE]


def unpack_kernel(blocks, out):
    for block in range(GROUP):
        out[:, block * WIDE : (block + 1) * WIDE] = blocks[block]


def shape(*sizes, dtype=F32):
    return jax.ShapeDtypeStruct(sizes, dtype)


def body(image_now, gradient, hessian_weight, psf_tiles, facet_of_row, tile_slot, thresholds):
    bands = 16
    band = lax.axis_index(BAND_AXES)
    place = jnp.stack([band, lax.axis_index(GROUP_AXES)]).astype(jnp.int32)
    sent = pl.pallas_call(
        pack_kernel,
        out_shape=shape(GROUP, SPLIT, LANES),
        in_specs=vmem(5),
        out_specs=vmem(1)[0],
        compiler_params=params(),
        name="pack",
    )(gradient, image_now, hessian_weight, psf_tiles, facet_of_row.reshape(SPLIT, 1))
    block = lax.all_to_all(sent, GROUP_AXES, split_axis=0, concat_axis=0, tiled=True)
    block = block.reshape(BAND, LANES)
    down = [(i, i + 1) for i in range(bands - 1)]
    up = [(i + 1, i) for i in range(bands - 1)]

    def halo(start, lanes, depth):
        return (
            lax.ppermute(block[BAND - depth :, start : start + lanes], BAND_AXES, down),
            lax.ppermute(block[:depth, start : start + lanes], BAND_AXES, up),
        )

    grad_halo = halo(G0, FRAME, DEEP)
    near_halo = halo(H0, FRAME + 128, NEAR)
    image_halo = halo(I0, FRAME, DEEP)
    own = block[:, T0:].reshape(GROUP, SPLIT, 128)[:, 0:2].transpose(1, 0, 2)
    tiles = lax.all_to_all(
        jnp.broadcast_to(own[None], (bands, 2, GROUP, 128)), BAND_AXES, split_axis=0, concat_axis=0, tiled=True
    )
    near = BAND + 2 * NEAR
    kept = BAND + 2 * MIDDLE
    deep = BAND + 2 * DEEP
    partial, forward, adjoint = pl.pallas_call(
        first_kernel,
        out_shape=(shape(256, 128), shape(near, 256), shape(kept, 256)),
        in_specs=vmem(7),
        out_specs=vmem(3),
        scratch_shapes=[
            pltpu.VMEM((deep, FRAME), F32),
            pltpu.VMEM((TILE, BAND, 768), BF16),
            pltpu.VMEM((768, FRAME), BF16),
            pltpu.VMEM((TILE * BAND, FRAME), F32),
        ],
        compiler_params=params(),
        name="first",
    )(block, *grad_halo, *near_halo, tiles, tile_slot.reshape(1, 256))

    def exchange(part):
        return lax.all_to_all(part, ALL_AXES, split_axis=0, concat_axis=0, tiled=True)

    sums = exchange(partial)
    partial, trial = pl.pallas_call(
        middle_kernel,
        out_shape=(shape(256, 128), shape(2, kept, FRAME)),
        in_specs=[smem(), smem(), *vmem(10)],
        out_specs=vmem(2),
        scratch_shapes=[
            pltpu.VMEM((deep, FRAME), F32),
            pltpu.VMEM((deep, FRAME), F32),
            pltpu.VMEM((near, FRAME), F32),
            pltpu.VMEM((deep + 2 * GUARD, FRAME), F32),
            pltpu.VMEM((deep + 2 * GUARD, FRAME), F32),
            pltpu.VMEM((deep, FRAME), F32),
            pltpu.VMEM((TILE, near, 768), BF16),
            pltpu.VMEM((768, FRAME), BF16),
            pltpu.VMEM((TILE * near, FRAME), F32),
            pltpu.VMEM((near, FRAME), F32),
        ],
        compiler_params=params(),
        name="middle",
    )(place, thresholds, block, *grad_halo, *image_halo, *near_halo, sums, forward, adjoint)
    sums = exchange(partial)
    result = pl.pallas_call(
        last_kernel,
        out_shape=shape(BAND, WIDE),
        in_specs=[smem(), smem(), *vmem(2)],
        out_specs=vmem(1)[0],
        scratch_shapes=[
            pltpu.VMEM((kept + 2 * GUARD, FRAME), F32),
            pltpu.VMEM((kept + 2 * GUARD, FRAME), F32),
            pltpu.VMEM((kept, FRAME), F32),
        ],
        compiler_params=params(),
        name="last",
    )(place, thresholds, trial, sums)
    blocks = lax.all_to_all(result.reshape(GROUP, SPLIT, WIDE), GROUP_AXES, split_axis=0, concat_axis=0, tiled=True)
    return pl.pallas_call(
        unpack_kernel,
        out_shape=shape(SPLIT, WIDE * GROUP),
        in_specs=vmem(1),
        out_specs=vmem(1)[0],
        compiler_params=params(),
        name="unpack",
    )(blocks)


def solution(mesh):
    fine = Mesh(mesh.devices.reshape(4, 4, 2, 2, 4), ALL_AXES)
    rows = P(ALL_AXES, None)
    in_specs = (rows, rows, rows, rows, P(ALL_AXES), P(), P())
    return jax.shard_map(body, mesh=fine, in_specs=in_specs, out_specs=rows, check_vma=False)
```

```python
import functools
import jax
import jax.numpy as jnp
from jax import lax
from jax.experimental import pallas as pl
from jax.experimental.pallas import tpu as pltpu
from jax.sharding import Mesh, PartitionSpec as P

TILE = 16
HALF = TILE // 2
LEVELS = 4
GROUP = 16
SPLIT = 8
BAND = GROUP * SPLIT
WIDE = 512
SIDE = 128
FRAME = WIDE + 2 * SIDE
DEEP = 80
NEAR = 40
MIDDLE = 32
REACH = 80
TILES = FRAME // 128
STRIP = 96
GUARD = 16
F32 = jnp.float32
BF16 = jnp.bfloat16

GROUP_AXES = ("zl", "core", "y")
BAND_AXES = ("x", "zh")
ALL_AXES = ("x", "zh", "zl", "core", "y")

G0, I0, H0, A0, T0 = 0, FRAME, 2 * FRAME, 3 * FRAME, 3 * FRAME + 128
LANES = T0 + 128


def params():
    return pltpu.CompilerParams(vmem_limit_bytes=56 * 1024 * 1024)


def vmem(count):
    return [pl.BlockSpec(memory_space=pltpu.VMEM)] * count


def smem():
    return pl.BlockSpec(memory_space=pltpu.SMEM)


def pack_kernel(grad, image, weight, tile, facet, out):
    columns = grad.shape[1]
    for start, source in ((G0, grad), (I0, image), (H0, weight)):
        for block in range(GROUP):
            low, high = block * WIDE - SIDE, block * WIDE + WIDE + SIDE
            left, right = max(0, -low), max(0, high - columns)
            if left:
                out[block, :, start : start + left] = jnp.zeros((SPLIT, left), F32)
            if right:
                out[block, :, start + FRAME - right : start + FRAME] = jnp.zeros((SPLIT, right), F32)
            out[block, :, start + left : start + FRAME - right] = source[:, low + left : high - right]
    row = iota((SPLIT, 128), 0)
    ids = jnp.zeros((SPLIT, 128), jnp.int32)
    for index in range(SPLIT):
        ids = jnp.where(row == index, facet[index] + 1, ids)
    ids = ids.astype(F32)
    halves = jnp.concatenate(
        [tile[:, 0:128], tile[:, 128:256], jnp.zeros((SPLIT - 2, 128), F32)], axis=0
    )
    for block in range(GROUP):
        out[block, :, A0 : A0 + 128] = ids
        out[block, :, T0 : T0 + 128] = halves


def split(value):
    high = value.astype(BF16)
    low = (value - high.astype(F32)).astype(BF16)
    return high, low


def iota(shape, dim):
    return lax.broadcasted_iota(jnp.int32, shape, dim)


def dot(a, b):
    return jnp.dot(a, b, preferred_element_type=F32)


def taps_of(ids, tiles, slots, orders):
    rows = ids.shape[0]
    facet = jnp.concatenate([ids, ids], axis=1)
    lane = iota((rows, 256), 1).astype(F32) + 1.0
    slot = jnp.sum(jnp.where(facet == lane, slots, 0.0), axis=1, keepdims=True)
    pick = (slot == lane).astype(F32).astype(BF16)
    row, col = iota((256, 256), 0), iota((256, 256), 1)
    parts = []
    for turned in orders:
        tap = 15 - col % 16 if turned else col % 16
        order = (row == tap * 16 + col // 16).astype(F32).astype(BF16)
        parts.append([dot(pick, dot(part, order).astype(BF16)) for part in split(tiles)])
    return parts


def table_of(tiles):
    return jnp.concatenate(
        [jnp.concatenate([tiles[g, half] for g in range(16)], axis=0) for half in range(2)], axis=1
    )


def turn(backward):
    kept = BAND + 2 * MIDDLE
    group = iota((kept, 256), 1) % 16
    value = backward[1 : 1 + kept]
    for step in range(1, TILE):
        value = jnp.where(group == step, backward[1 + step : 1 + step + kept], value)
    return value


def banded(taps, start, rows, offset, out):
    size = 16
    for part in range(rows // size):
        first = start + part * size
        place = iota((size, 256), 1) - iota((size, 256), 0) - (offset + part * size)
        bands = [(place >= p * REACH) & (place < p * REACH + TILE) for p in range(3)]
        skews = [
            pltpu.roll(taps[p, pl.ds(first, size), :], offset + part * size, 1, stride=1, stride_axis=0) for p in range(2)
        ]
        made = {}

        def rolled(which, turns):
            turns %= 16
            if (which, turns) not in made:
                made[which, turns] = pltpu.roll(skews[which], 16 * turns, 1) if turns else skews[which]
            return made[which, turns]

        for column in range(TILE):
            matrix = jnp.where(bands[2], rolled(1, 10 - column), 0.0)
            matrix = jnp.where(bands[1], rolled(0, 5 - column), matrix)
            matrix = jnp.where(bands[0], rolled(0, -column), matrix)
            out[column * rows + part * size : column * rows + (part + 1) * size, :] = matrix.astype(BF16)


def put_operand(value, pieces):
    rows = value.shape[0]
    high, low = split(value)
    for place, part in ((0, high), (REACH, low), (2 * REACH, high)):
        pieces[place : place + rows, :] = part
        if rows < REACH:
            pieces[place + rows : place + REACH, :] = jnp.zeros((REACH - rows, FRAME), BF16)
    pieces[3 * REACH : 256, :] = jnp.zeros((256 - 3 * REACH, FRAME), BF16)


def blur(taps, start, rows, value, ahead, matrix, pieces, planes, emit):
    put_operand(value, pieces)
    banded(taps, start, rows, 0 if ahead else 1, matrix)
    planes[0 : TILE * rows, :] = dot(matrix[0 : TILE * rows, :], pieces[...])

    def total(at, first, count):
        if count == 1:
            return planes[first * rows + at : first * rows + at + 8, :]
        half = count // 2
        left = total(at, first, half)
        right = total(at, first + half, half)
        return left + pltpu.roll(right, FRAME - half if ahead else half, 1)

    for at in range(0, rows, 8):
        emit(at, pltpu.roll(total(at, 0, TILE), HALF if ahead else FRAME - HALF, 1))


def edges(band, block):
    return (block > 0).astype(F32), (block < GROUP - 1).astype(F32)


def row_inside(first, band):
    row = first + band * BAND
    return ((row >= 0) & (row < BAND * 16)).astype(F32)


def starlet(planes, total, spans, top, limits, band, sides):
    lane = iota((8, 128), 1)

    def level(depth):
        source, target = planes[depth % 2], planes[1 - depth % 2]
        d = 2**depth
        limit = limits[depth]
        begin, end = spans[depth]

        def rows_from(start):
            inside = row_inside(top + start, band)
            edge, near, mid = 0.0625 * inside, 0.25 * inside, 0.375 * inside

            def at(t, offset):
                return source[t, pl.ds(start + GUARD + offset, 8), :]

            plain = [at(t, 0) for t in range(TILES)]
            down = [
                edge * (at(t, -2 * d) + at(t, 2 * d)) + near * (at(t, -d) + at(t, d)) + mid * plain[t]
                for t in range(TILES)
            ]

            def moved(s):
                right = [pltpu.roll(v, s, 1) for v in down]
                left = [pltpu.roll(v, 128 - s, 1) for v in down]
                return [
                    jnp.where(lane < s, right[max(t - 1, 0)], right[t])
                    + jnp.where(lane >= 128 - s, left[min(t + 1, TILES - 1)], left[t])
                    for t in range(TILES)
                ]

            outer, inner = moved(2 * d), moved(d)
            result = []
            for t in range(TILES):
                smoother = 0.0625 * outer[t] + 0.25 * inner[t] + 0.375 * down[t]
                if t == 0:
                    smoother = smoother * sides[0]
                if t == TILES - 1:
                    smoother = smoother * sides[1]
                cut = jnp.clip(plain[t] - smoother, -limit, limit)
                before = total[t, pl.ds(start, 8), :] if depth else plain[t]
                result.append((smoother, before - cut))
            return result

        def chunk(index, carry):
            start = pl.multiple_of(begin + index * STRIP, 8)
            results = [(start + at, rows_from(start + at)) for at in range(0, STRIP, 8)]
            for first, result in results:
                for t in range(TILES):
                    if depth < LEVELS - 1:
                        target[t, pl.ds(first + GUARD, 8), :] = result[t][0]
                    total[t, pl.ds(first, 8), :] = result[t][1]
            return carry

        assert (end - begin) % STRIP == 0
        lax.fori_loop(0, (end - begin) // STRIP, chunk, 0)

    for depth in range(LEVELS):
        level(depth)


def clear_guards(plane, rows):
    plane[:, 0:GUARD, :] = jnp.zeros((TILES, GUARD, 128), F32)
    plane[:, GUARD + rows : 2 * GUARD + rows, :] = jnp.zeros((TILES, GUARD, 128), F32)


def put_partials(out, numerator, denominator):
    lane = iota((256, 128), 1)
    out[...] = jnp.where(lane == 0, numerator, jnp.where(lane == 1, denominator, 0.0))


def step_of(sums):
    total = jnp.sum(sums[...], axis=0, keepdims=True)
    lane = iota((1, 128), 1)
    return jnp.sum(jnp.where(lane == 0, total, 0.0)) / jnp.sum(jnp.where(lane == 1, total, 0.0))


def weigh_tile(taps, start, values, weights, operand, matrix, pieces, planes, sums):
    carry = [sums[0], sums[1]]

    def weigh(at, blurred):
        value, heavy = values(at), weights(at)
        blurred = blurred[:, SIDE : SIDE + WIDE]
        carry[:] = carry[0] + value * value, carry[1] + heavy * blurred * blurred

    blur(taps, start, 64, operand, True, matrix, pieces, planes, weigh)
    sums[0] = carry[0]
    sums[1] = carry[1]


def first_kernel(block, grad_up, grad_down, tiles, slots, partial, grad, matrix, pieces, planes, forward, sums):
    taps = taps_of(block[:, A0 : A0 + 128], table_of(tiles), slots[...].astype(F32) + 1.0, (False,))[0]
    for part in range(2):
        forward[part] = taps[part]
    grad[0:HALF, :] = grad_up[...]
    grad[HALF : HALF + BAND, :] = block[:, G0 : G0 + FRAME]
    grad[HALF + BAND : 2 * HALF + BAND, :] = grad_down[...]
    sums[...] = jnp.zeros((2, 8, WIDE), F32)

    def tile(index, carry):
        start = pl.multiple_of(index * 64, 64)
        weigh_tile(
            forward,
            start,
            lambda at: block[pl.ds(start + at, 8), G0 + SIDE : G0 + SIDE + WIDE],
            lambda at: block[pl.ds(start + at, 8), H0 + SIDE : H0 + SIDE + WIDE],
            grad[pl.ds(start, REACH), :],
            matrix, pieces, planes, sums,
        )
        return carry

    lax.fori_loop(0, BAND // 64, tile, 0)
    put_partials(partial, jnp.sum(sums[0]), jnp.sum(sums[1]))


def middle_kernel(
    place, thresholds, block, above, below, totals, tiles, slots,
    partial, trial,
    grad, image, weight, plane_a, plane_b, total, matrix, pieces, planes, pushed, forward, adjoint, sums,
):
    band, sides = place[0], edges(place[0], place[1])
    rows = BAND + 2 * DEEP
    near = BAND + 2 * NEAR
    kept = BAND + 2 * MIDDLE
    step = step_of(totals)
    for start, lane, target in ((0, G0, grad), (0, I0, image), (DEEP - NEAR, H0, weight)):
        depth = DEEP - start
        target[0:depth, :] = above[start:DEEP, lane : lane + FRAME]
        target[depth : depth + BAND, :] = block[:, lane : lane + FRAME]
        target[depth + BAND : 2 * depth + BAND, :] = below[0:depth, lane : lane + FRAME]
    ids = jnp.concatenate([part[:, A0 : A0 + 128] for part in (above[DEEP - NEAR : DEEP, :], block[...], below[0:NEAR, :])], axis=0)
    ahead, back = taps_of(ids, table_of(tiles), slots[...].astype(F32) + 1.0, (False, True))
    for part in range(2):
        forward[part] = ahead[part]
        adjoint[part] = turn(back[part])
    clear_guards(plane_a, rows)
    clear_guards(plane_b, rows)
    for t in range(TILES):
        lanes = slice(128 * t, 128 * t + 128)
        plane_a[t, GUARD : GUARD + rows, :] = image[:, lanes] - step * grad[:, lanes]
    limits = [step * thresholds[k] for k in range(LEVELS)]
    spans = ((0, 288),) * LEVELS
    starlet((plane_a, plane_b), total, spans, -DEEP, limits, band, sides)

    def change(first, count):
        new = jnp.concatenate([total[t, pl.ds(first, count), :] for t in range(TILES)], axis=1)
        return new - image[pl.ds(first, count), :]

    def push_tile(index, carry):
        start = pl.multiple_of(jnp.minimum(index * 64, near - 64), 16)

        def push(at, blurred):
            pushed[pl.ds(start + at, 8), :] = weight[pl.ds(start + at, 8), :] * blurred

        value = change(start + (DEEP - NEAR - HALF), REACH)
        blur(forward, start, 64, value, True, matrix, pieces, planes, push)
        return carry

    lax.fori_loop(0, 4, push_tile, 0)

    def descend_tile(index, carry):
        start = pl.multiple_of(index * 64, 64)

        def descend(at, spread):
            inside = row_inside(start + (at - MIDDLE), band)
            value = (grad[pl.ds(start + (at + DEEP - MIDDLE), 8), :] + spread) * inside
            for t in range(TILES):
                lanes = slice(128 * t, 128 * t + 128)
                part = value[:, lanes]
                if t == 0:
                    part = part * sides[0]
                if t == TILES - 1:
                    part = part * sides[1]
                trial[1, pl.ds(start + at, 8), lanes] = part

        blur(adjoint, start, 64, pushed[pl.ds(start, REACH), :], False, matrix, pieces, planes, descend)
        return carry

    lax.fori_loop(0, kept // 64, descend_tile, 0)
    for t in range(TILES):
        trial[0, :, 128 * t : 128 * t + 128] = total[t, DEEP - MIDDLE : DEEP - MIDDLE + kept, :]

    sums[...] = jnp.zeros((2, 8, WIDE), F32)

    def last_tile(index, carry):
        start = pl.multiple_of(index * 64, 64)
        weigh_tile(
            forward,
            start + NEAR,
            lambda at: trial[1, pl.ds(start + (at + MIDDLE), 8), SIDE : SIDE + WIDE],
            lambda at: weight[pl.ds(start + (at + NEAR), 8), SIDE : SIDE + WIDE],
            trial[1, pl.ds(start + (MIDDLE - HALF), REACH), :],
            matrix, pieces, planes, sums,
        )
        return carry

    lax.fori_loop(0, BAND // 64, last_tile, 0)
    put_partials(partial, jnp.sum(sums[0]), jnp.sum(sums[1]))


def last_kernel(place, thresholds, trial, sums, out, plane_a, plane_b, total):
    step = step_of(sums)
    rows = BAND + 2 * MIDDLE
    clear_guards(plane_a, rows)
    clear_guards(plane_b, rows)
    for t in range(TILES):
        lanes = slice(128 * t, 128 * t + 128)
        plane_a[t, GUARD : GUARD + rows, :] = trial[0, :, lanes] - step * trial[1, :, lanes]
    limits = [step * thresholds[k] for k in range(LEVELS)]
    spans = ((0, 192),) * LEVELS
    starlet((plane_a, plane_b), total, spans, -MIDDLE, limits, place[0], edges(place[0], place[1]))
    for t in range(WIDE // 128):
        out[:, 128 * t : 128 * t + 128] = total[t + 1, MIDDLE : MIDDLE + BAND, :]


def unpack_kernel(blocks, out):
    for block in range(GROUP):
        out[:, block * WIDE : (block + 1) * WIDE] = blocks[block]


def shape(*sizes, dtype=F32):
    return jax.ShapeDtypeStruct(sizes, dtype)


def body(image_now, gradient, hessian_weight, psf_tiles, facet_of_row, tile_slot, thresholds):
    bands = 16
    band = lax.axis_index(BAND_AXES)
    place = jnp.stack([band, lax.axis_index(GROUP_AXES)]).astype(jnp.int32)
    sent = pl.pallas_call(
        pack_kernel,
        out_shape=shape(GROUP, SPLIT, LANES),
        in_specs=[*vmem(4), smem()],
        out_specs=vmem(1)[0],
        compiler_params=params(),
        name="pack",
    )(gradient, image_now, hessian_weight, psf_tiles, facet_of_row)
    block = lax.all_to_all(sent, GROUP_AXES, split_axis=0, concat_axis=0, tiled=True)
    block = block.reshape(BAND, LANES)
    down = [(i, i + 1) for i in range(bands - 1)]
    up = [(i + 1, i) for i in range(bands - 1)]

    above = lax.ppermute(block[BAND - DEEP :], BAND_AXES, down)
    below = lax.ppermute(block[:DEEP], BAND_AXES, up)
    own = block[:, T0:].reshape(GROUP, SPLIT, 128)[:, 0:2].transpose(1, 0, 2)
    tiles = lax.all_to_all(
        jnp.broadcast_to(own[None], (bands, 2, GROUP, 128)), BAND_AXES, split_axis=0, concat_axis=0, tiled=True
    )
    near = BAND + 2 * NEAR
    kept = BAND + 2 * MIDDLE
    deep = BAND + 2 * DEEP
    slots = tile_slot.reshape(1, 256)
    partial = pl.pallas_call(
        first_kernel,
        grid=(1,),
        out_shape=shape(256, 128),
        in_specs=[
            *vmem(1),
            pl.BlockSpec((HALF, FRAME), lambda i: (DEEP // HALF - 1, 0)),
            pl.BlockSpec((HALF, FRAME), lambda i: (0, 0)),
            *vmem(2),
        ],
        out_specs=vmem(1)[0],
        scratch_shapes=[
            pltpu.VMEM((BAND + 2 * HALF, FRAME), F32),
            pltpu.VMEM((TILE * 64, 256), BF16),
            pltpu.VMEM((256, FRAME), BF16),
            pltpu.VMEM((TILE * 64, FRAME), F32),
            pltpu.VMEM((2, BAND, 256), F32),
            pltpu.VMEM((2, 8, WIDE), F32),
        ],
        compiler_params=params(),
        name="first",
    )(block, above, below, tiles, slots)

    def exchange(part):
        return lax.all_to_all(part, ALL_AXES, split_axis=0, concat_axis=0, tiled=True)

    sums = exchange(partial)
    partial, trial = pl.pallas_call(
        middle_kernel,
        out_shape=(shape(256, 128), shape(2, kept, FRAME)),
        in_specs=[smem(), smem(), *vmem(6)],
        out_specs=vmem(2),
        scratch_shapes=[
            pltpu.VMEM((deep, FRAME), F32),
            pltpu.VMEM((deep, FRAME), F32),
            pltpu.VMEM((near, FRAME), F32),
            pltpu.VMEM((TILES, deep + 2 * GUARD, 128), F32),
            pltpu.VMEM((TILES, deep + 2 * GUARD, 128), F32),
            pltpu.VMEM((TILES, deep, 128), F32),
            pltpu.VMEM((TILE * 64, 256), BF16),
            pltpu.VMEM((256, FRAME), BF16),
            pltpu.VMEM((TILE * 64, FRAME), F32),
            pltpu.VMEM((near, FRAME), F32),
            pltpu.VMEM((2, near, 256), F32),
            pltpu.VMEM((2, kept, 256), F32),
            pltpu.VMEM((2, 8, WIDE), F32),
        ],
        compiler_params=params(),
        name="middle",
    )(place, thresholds, block, above, below, sums, tiles, slots)
    sums = exchange(partial)
    result = pl.pallas_call(
        last_kernel,
        out_shape=shape(BAND, WIDE),
        in_specs=[smem(), smem(), *vmem(2)],
        out_specs=vmem(1)[0],
        scratch_shapes=[
            pltpu.VMEM((TILES, kept + 2 * GUARD, 128), F32),
            pltpu.VMEM((TILES, kept + 2 * GUARD, 128), F32),
            pltpu.VMEM((TILES, kept, 128), F32),
        ],
        compiler_params=params(),
        name="last",
    )(place, thresholds, trial, sums)
    blocks = lax.all_to_all(result.reshape(GROUP, SPLIT, WIDE), GROUP_AXES, split_axis=0, concat_axis=0, tiled=True)
    return pl.pallas_call(
        unpack_kernel,
        out_shape=shape(SPLIT, WIDE * GROUP),
        in_specs=vmem(1),
        out_specs=vmem(1)[0],
        compiler_params=params(),
        name="unpack",
    )(blocks)


def solution(mesh):
    fine = Mesh(mesh.devices.reshape(4, 4, 2, 2, 4), ALL_AXES)
    rows = P(ALL_AXES, None)
    in_specs = (rows, rows, rows, rows, P(ALL_AXES), P(), P())
    return jax.shard_map(body, mesh=fine, in_specs=in_specs, out_specs=rows, check_vma=False)
```

```python
import functools
import jax
import jax.numpy as jnp
from jax import lax
from jax.experimental import pallas as pl
from jax.experimental.pallas import tpu as pltpu
from jax.sharding import Mesh, PartitionSpec as P

TILE = 16
HALF = TILE // 2
LEVELS = 4
GROUP = 16
SPLIT = 8
BAND = GROUP * SPLIT
WIDE = 512
SIDE = 128
FRAME = WIDE + 2 * SIDE
DEEP = 80
NEAR = 40
MIDDLE = 32
REACH = 80
TILES = FRAME // 128
STRIP = 96
GUARD = 16
F32 = jnp.float32
BF16 = jnp.bfloat16

GROUP_AXES = ("zl", "core", "y")
BAND_AXES = ("x", "zh")
ALL_AXES = ("x", "zh", "zl", "core", "y")

G0, I0, H0, T0 = 0, FRAME, 2 * FRAME, 3 * FRAME
FACET = FRAME - 1
LANES = T0 + 128


def params():
    return pltpu.CompilerParams(vmem_limit_bytes=56 * 1024 * 1024)


def vmem(count):
    return [pl.BlockSpec(memory_space=pltpu.VMEM)] * count


def smem():
    return pl.BlockSpec(memory_space=pltpu.SMEM)


def pack_kernel(grad, image, weight, tile, facet, out):
    columns = grad.shape[1]
    for start, source in ((G0, grad), (I0, image), (H0, weight)):
        for block in range(GROUP):
            low, high = block * WIDE - SIDE, block * WIDE + WIDE + SIDE
            left, right = max(0, -low), max(0, high - columns)
            if left:
                out[block, :, start : start + left] = jnp.zeros((SPLIT, left), F32)
            if right:
                out[block, :, start + FRAME - right : start + FRAME] = jnp.zeros((SPLIT, right), F32)
            out[block, :, start + left : start + FRAME - right] = source[:, low + left : high - right]
    row, lane = iota((SPLIT, 128), 0), iota((SPLIT, 128), 1)
    ids = jnp.zeros((SPLIT, 128), jnp.int32)
    for index in range(SPLIT):
        ids = jnp.where(row == index, facet[index] + 1, ids)
    ids = ids.astype(F32)
    halves = jnp.concatenate(
        [tile[:, 0:128], tile[:, 128:256], jnp.zeros((SPLIT - 2, 128), F32)], axis=0
    )
    for block in range(GROUP):
        tail = out[block, :, T0 - 128 : T0]
        out[block, :, T0 - 128 : T0] = jnp.where(lane == 127, ids, tail)
        out[block, :, T0 : T0 + 128] = halves


def split(value):
    high = value.astype(BF16)
    low = (value - high.astype(F32)).astype(BF16)
    return high, low


def iota(shape, dim):
    return lax.broadcasted_iota(jnp.int32, shape, dim)


def dot(a, b):
    return jnp.dot(a, b, preferred_element_type=F32)


def taps_of(ids, tiles, slots, orders):
    rows = ids.shape[0]
    facet = jnp.broadcast_to(ids, (rows, 256))
    lane = iota((rows, 256), 1).astype(F32) + 1.0
    slot = jnp.sum(jnp.where(facet == lane, slots, 0.0), axis=1, keepdims=True)
    pick = (slot == lane).astype(F32).astype(BF16)
    row, col = iota((256, 256), 0), iota((256, 256), 1)
    parts = []
    for turned in orders:
        tap = 15 - col % 16 if turned else col % 16
        order = (row == tap * 16 + col // 16).astype(F32).astype(BF16)
        parts.append([dot(pick, dot(part, order).astype(BF16)) for part in split(tiles)])
    return parts


def table_of(tiles):
    return jnp.concatenate(
        [jnp.concatenate([tiles[g, half] for g in range(16)], axis=0) for half in range(2)], axis=1
    )


def turn(backward):
    kept = BAND + 2 * MIDDLE
    group = iota((kept, 256), 1) % 16
    value = backward[1 : 1 + kept]
    for step in range(1, TILE):
        value = jnp.where(group == step, backward[1 + step : 1 + step + kept], value)
    return value


def banded(taps, start, rows, offset, out):
    size = 16
    for part in range(rows // size):
        first = start + part * size
        place = iota((size, 256), 1) - iota((size, 256), 0) - (offset + part * size)
        bands = [(place >= p * REACH) & (place < p * REACH + TILE) for p in range(3)]
        skews = [
            pltpu.roll(taps[p, pl.ds(first, size), :], offset + part * size, 1, stride=1, stride_axis=0) for p in range(2)
        ]
        made = {}

        def rolled(which, turns):
            turns %= 16
            if (which, turns) not in made:
                made[which, turns] = pltpu.roll(skews[which], 16 * turns, 1) if turns else skews[which]
            return made[which, turns]

        for column in range(TILE):
            matrix = jnp.where(bands[2], rolled(1, 10 - column), 0.0)
            matrix = jnp.where(bands[1], rolled(0, 5 - column), matrix)
            matrix = jnp.where(bands[0], rolled(0, -column), matrix)
            out[column * rows + part * size : column * rows + (part + 1) * size, :] = matrix.astype(BF16)


def put_operand(value, pieces):
    rows = value.shape[0]
    high, low = split(value)
    for place, part in ((0, high), (REACH, low), (2 * REACH, high)):
        pieces[place : place + rows, :] = part
        if rows < REACH:
            pieces[place + rows : place + REACH, :] = jnp.zeros((REACH - rows, FRAME), BF16)
    pieces[3 * REACH : 256, :] = jnp.zeros((256 - 3 * REACH, FRAME), BF16)


def blur(taps, start, rows, value, ahead, matrix, pieces, planes, emit):
    put_operand(value, pieces)
    banded(taps, start, rows, 0 if ahead else 1, matrix)
    planes[0 : TILE * rows, :] = dot(matrix[0 : TILE * rows, :], pieces[...])

    def total(at, first, count):
        if count == 1:
            return planes[first * rows + at : first * rows + at + 8, :]
        half = count // 2
        left = total(at, first, half)
        right = total(at, first + half, half)
        return left + pltpu.roll(right, FRAME - half if ahead else half, 1)

    for at in range(0, rows, 8):
        emit(at, pltpu.roll(total(at, 0, TILE), HALF if ahead else FRAME - HALF, 1))


def edges(band, block):
    return (block > 0).astype(F32), (block < GROUP - 1).astype(F32)


def row_inside(first, band):
    row = first + band * BAND
    return ((row >= 0) & (row < BAND * 16)).astype(F32)


def starlet(planes, total, spans, top, limits, band, sides):
    lane = iota((8, 128), 1)

    def level(depth):
        source, target = planes[depth % 2], planes[1 - depth % 2]
        d = 2**depth
        limit = limits[depth]
        begin, end = spans[depth]

        def rows_from(start):
            inside = row_inside(top + start, band)
            edge, near, mid = 0.0625 * inside, 0.25 * inside, 0.375 * inside

            def at(t, offset):
                return source[t, pl.ds(start + GUARD + offset, 8), :]

            plain = [at(t, 0) for t in range(TILES)]
            down = [
                edge * (at(t, -2 * d) + at(t, 2 * d)) + near * (at(t, -d) + at(t, d)) + mid * plain[t]
                for t in range(TILES)
            ]

            def moved(s):
                right = [pltpu.roll(v, s, 1) for v in down]
                left = [pltpu.roll(v, 128 - s, 1) for v in down]
                return [
                    jnp.where(lane < s, right[max(t - 1, 0)], right[t])
                    + jnp.where(lane >= 128 - s, left[min(t + 1, TILES - 1)], left[t])
                    for t in range(TILES)
                ]

            outer, inner = moved(2 * d), moved(d)
            result = []
            for t in range(TILES):
                smoother = 0.0625 * outer[t] + 0.25 * inner[t] + 0.375 * down[t]
                if t == 0:
                    smoother = smoother * sides[0]
                if t == TILES - 1:
                    smoother = smoother * sides[1]
                cut = jnp.clip(plain[t] - smoother, -limit, limit)
                before = total[t, pl.ds(start, 8), :] if depth else plain[t]
                result.append((smoother, before - cut))
            return result

        def chunk(index, carry):
            start = pl.multiple_of(begin + index * STRIP, 8)
            results = [(start + at, rows_from(start + at)) for at in range(0, STRIP, 8)]
            for first, result in results:
                for t in range(TILES):
                    if depth < LEVELS - 1:
                        target[t, pl.ds(first + GUARD, 8), :] = result[t][0]
                    total[t, pl.ds(first, 8), :] = result[t][1]
            return carry

        assert (end - begin) % STRIP == 0
        lax.fori_loop(0, (end - begin) // STRIP, chunk, 0)

    for depth in range(LEVELS):
        level(depth)


def clear_guards(plane, rows):
    plane[:, 0:GUARD, :] = jnp.zeros((TILES, GUARD, 128), F32)
    plane[:, GUARD + rows : 2 * GUARD + rows, :] = jnp.zeros((TILES, GUARD, 128), F32)


def put_partials(out, numerator, denominator):
    lane = iota((256, 128), 1)
    out[...] = jnp.where(lane == 0, numerator, jnp.where(lane == 1, denominator, 0.0))


def step_of(sums):
    total = jnp.sum(sums[...], axis=0, keepdims=True)
    lane = iota((1, 128), 1)
    return jnp.sum(jnp.where(lane == 0, total, 0.0)) / jnp.sum(jnp.where(lane == 1, total, 0.0))


def weigh_tile(taps, start, values, weights, operand, matrix, pieces, planes, sums):
    carry = [sums[0], sums[1]]

    def weigh(at, blurred):
        value, heavy = values(at), weights(at)
        blurred = blurred[:, SIDE : SIDE + WIDE]
        carry[:] = carry[0] + value * value, carry[1] + heavy * blurred * blurred

    blur(taps, start, 64, operand, True, matrix, pieces, planes, weigh)
    sums[0] = carry[0]
    sums[1] = carry[1]


def first_kernel(block, grad_up, grad_down, tiles, slots, partial, grad, matrix, pieces, planes, forward, sums):
    taps = taps_of(block[:, H0 + FACET : H0 + FRAME], table_of(tiles), slots[...].astype(F32) + 1.0, (False,))[0]
    for part in range(2):
        forward[part] = taps[part]
    grad[0:HALF, :] = grad_up[...]
    grad[HALF : HALF + BAND, :] = block[:, G0 : G0 + FRAME]
    grad[HALF + BAND : 2 * HALF + BAND, :] = grad_down[...]
    sums[...] = jnp.zeros((2, 8, WIDE), F32)

    def tile(index, carry):
        start = pl.multiple_of(index * 64, 64)
        weigh_tile(
            forward,
            start,
            lambda at: block[pl.ds(start + at, 8), G0 + SIDE : G0 + SIDE + WIDE],
            lambda at: block[pl.ds(start + at, 8), H0 + SIDE : H0 + SIDE + WIDE],
            grad[pl.ds(start, REACH), :],
            matrix, pieces, planes, sums,
        )
        return carry

    lax.fori_loop(0, BAND // 64, tile, 0)
    put_partials(partial, jnp.sum(sums[0]), jnp.sum(sums[1]))


def middle_kernel(
    place, thresholds, block, grad_up, grad_down, other_up, other_down, totals, tiles, slots,
    partial, trial,
    grad, image, weight, plane_a, plane_b, total, matrix, pieces, planes, pushed, forward, adjoint, sums,
):
    band, sides = place[0], edges(place[0], place[1])
    rows = BAND + 2 * DEEP
    near = BAND + 2 * NEAR
    kept = BAND + 2 * MIDDLE
    step = step_of(totals)
    for depth, start, lane, target, up, down in (
        (DEEP, 0, G0, grad, grad_up, grad_down),
        (DEEP, 0, I0, image, other_up, other_down),
        (NEAR, DEEP, H0, weight, other_up, other_down),
    ):
        target[0:depth, :] = up[start : start + depth, :]
        target[depth : depth + BAND, :] = block[:, lane : lane + FRAME]
        target[depth + BAND : 2 * depth + BAND, :] = down[start : start + depth, :]
    ids = weight[:, FACET:FRAME]
    ahead, back = taps_of(ids, table_of(tiles), slots[...].astype(F32) + 1.0, (False, True))
    for part in range(2):
        forward[part] = ahead[part]
        adjoint[part] = turn(back[part])
    clear_guards(plane_a, rows)
    clear_guards(plane_b, rows)
    for t in range(TILES):
        lanes = slice(128 * t, 128 * t + 128)
        plane_a[t, GUARD : GUARD + rows, :] = image[:, lanes] - step * grad[:, lanes]
    limits = [step * thresholds[k] for k in range(LEVELS)]
    spans = ((0, 288),) * LEVELS
    starlet((plane_a, plane_b), total, spans, -DEEP, limits, band, sides)

    def change(first, count):
        new = jnp.concatenate([total[t, pl.ds(first, count), :] for t in range(TILES)], axis=1)
        return new - image[pl.ds(first, count), :]

    def push_tile(index, carry):
        start = pl.multiple_of(jnp.minimum(index * 64, near - 64), 16)

        def push(at, blurred):
            pushed[pl.ds(start + at, 8), :] = weight[pl.ds(start + at, 8), :] * blurred

        value = change(start + (DEEP - NEAR - HALF), REACH)
        blur(forward, start, 64, value, True, matrix, pieces, planes, push)
        return carry

    lax.fori_loop(0, 4, push_tile, 0)

    def descend_tile(index, carry):
        start = pl.multiple_of(index * 64, 64)

        def descend(at, spread):
            inside = row_inside(start + (at - MIDDLE), band)
            value = (grad[pl.ds(start + (at + DEEP - MIDDLE), 8), :] + spread) * inside
            for t in range(TILES):
                lanes = slice(128 * t, 128 * t + 128)
                part = value[:, lanes]
                if t == 0:
                    part = part * sides[0]
                if t == TILES - 1:
                    part = part * sides[1]
                trial[1, pl.ds(start + at, 8), lanes] = part

        blur(adjoint, start, 64, pushed[pl.ds(start, REACH), :], False, matrix, pieces, planes, descend)
        return carry

    lax.fori_loop(0, kept // 64, descend_tile, 0)
    for t in range(TILES):
        trial[0, :, 128 * t : 128 * t + 128] = total[t, DEEP - MIDDLE : DEEP - MIDDLE + kept, :]

    sums[...] = jnp.zeros((2, 8, WIDE), F32)

    def last_tile(index, carry):
        start = pl.multiple_of(index * 64, 64)
        weigh_tile(
            forward,
            start + NEAR,
            lambda at: trial[1, pl.ds(start + (at + MIDDLE), 8), SIDE : SIDE + WIDE],
            lambda at: weight[pl.ds(start + (at + NEAR), 8), SIDE : SIDE + WIDE],
            trial[1, pl.ds(start + (MIDDLE - HALF), REACH), :],
            matrix, pieces, planes, sums,
        )
        return carry

    lax.fori_loop(0, BAND // 64, last_tile, 0)
    put_partials(partial, jnp.sum(sums[0]), jnp.sum(sums[1]))


def last_kernel(place, thresholds, trial, sums, out, plane_a, plane_b, total):
    step = step_of(sums)
    rows = BAND + 2 * MIDDLE
    clear_guards(plane_a, rows)
    clear_guards(plane_b, rows)
    for t in range(TILES):
        lanes = slice(128 * t, 128 * t + 128)
        plane_a[t, GUARD : GUARD + rows, :] = trial[0, :, lanes] - step * trial[1, :, lanes]
    limits = [step * thresholds[k] for k in range(LEVELS)]
    spans = ((0, 192),) * LEVELS
    starlet((plane_a, plane_b), total, spans, -MIDDLE, limits, place[0], edges(place[0], place[1]))
    for t in range(WIDE // 128):
        out[:, 128 * t : 128 * t + 128] = total[t + 1, MIDDLE : MIDDLE + BAND, :]


def unpack_kernel(blocks, out):
    for block in range(GROUP):
        out[:, block * WIDE : (block + 1) * WIDE] = blocks[block]


def shape(*sizes, dtype=F32):
    return jax.ShapeDtypeStruct(sizes, dtype)


def body(image_now, gradient, hessian_weight, psf_tiles, facet_of_row, tile_slot, thresholds):
    bands = 16
    band = lax.axis_index(BAND_AXES)
    place = jnp.stack([band, lax.axis_index(GROUP_AXES)]).astype(jnp.int32)
    sent = pl.pallas_call(
        pack_kernel,
        out_shape=shape(GROUP, SPLIT, LANES),
        in_specs=[*vmem(4), smem()],
        out_specs=vmem(1)[0],
        compiler_params=params(),
        name="pack",
    )(gradient, image_now, hessian_weight, psf_tiles, facet_of_row)
    block = lax.all_to_all(sent, GROUP_AXES, split_axis=0, concat_axis=0, tiled=True)
    block = block.reshape(BAND, LANES)
    down = [(i, i + 1) for i in range(bands - 1)]
    up = [(i + 1, i) for i in range(bands - 1)]

    grad_up = lax.ppermute(block[BAND - DEEP :, G0 : G0 + FRAME], BAND_AXES, down)
    grad_down = lax.ppermute(block[:DEEP, G0 : G0 + FRAME], BAND_AXES, up)
    later, grad_down = lax.optimization_barrier((block, grad_down))
    bottom = jnp.concatenate([later[BAND - DEEP :, I0:H0], later[BAND - NEAR :, H0:T0]])
    top = jnp.concatenate([later[:DEEP, I0:H0], later[:NEAR, H0:T0]])
    other_up = lax.ppermute(bottom, BAND_AXES, down)
    other_down = lax.ppermute(top, BAND_AXES, up)
    own = block[:, T0:].reshape(GROUP, SPLIT, 128)[:, 0:2].transpose(1, 0, 2)
    tiles = lax.all_to_all(
        jnp.broadcast_to(own[None], (bands, 2, GROUP, 128)), BAND_AXES, split_axis=0, concat_axis=0, tiled=True
    )
    near = BAND + 2 * NEAR
    kept = BAND + 2 * MIDDLE
    deep = BAND + 2 * DEEP
    slots = tile_slot.reshape(1, 256)
    partial = pl.pallas_call(
        first_kernel,
        grid=(1,),
        out_shape=shape(256, 128),
        in_specs=[
            *vmem(1),
            pl.BlockSpec((HALF, FRAME), lambda i: (DEEP // HALF - 1, 0)),
            pl.BlockSpec((HALF, FRAME), lambda i: (0, 0)),
            *vmem(2),
        ],
        out_specs=vmem(1)[0],
        scratch_shapes=[
            pltpu.VMEM((BAND + 2 * HALF, FRAME), F32),
            pltpu.VMEM((TILE * 64, 256), BF16),
            pltpu.VMEM((256, FRAME), BF16),
            pltpu.VMEM((TILE * 64, FRAME), F32),
            pltpu.VMEM((2, BAND, 256), F32),
            pltpu.VMEM((2, 8, WIDE), F32),
        ],
        compiler_params=params(),
        name="first",
    )(block, grad_up, grad_down, tiles, slots)

    def exchange(part):
        return lax.all_to_all(part, ALL_AXES, split_axis=0, concat_axis=0, tiled=True)

    sums = exchange(partial)
    partial, trial = pl.pallas_call(
        middle_kernel,
        out_shape=(shape(256, 128), shape(2, kept, FRAME)),
        in_specs=[smem(), smem(), *vmem(8)],
        out_specs=vmem(2),
        scratch_shapes=[
            pltpu.VMEM((deep, FRAME), F32),
            pltpu.VMEM((deep, FRAME), F32),
            pltpu.VMEM((near, FRAME), F32),
            pltpu.VMEM((TILES, deep + 2 * GUARD, 128), F32),
            pltpu.VMEM((TILES, deep + 2 * GUARD, 128), F32),
            pltpu.VMEM((TILES, deep, 128), F32),
            pltpu.VMEM((TILE * 64, 256), BF16),
            pltpu.VMEM((256, FRAME), BF16),
            pltpu.VMEM((TILE * 64, FRAME), F32),
            pltpu.VMEM((near, FRAME), F32),
            pltpu.VMEM((2, near, 256), F32),
            pltpu.VMEM((2, kept, 256), F32),
            pltpu.VMEM((2, 8, WIDE), F32),
        ],
        compiler_params=params(),
        name="middle",
    )(place, thresholds, block, grad_up, grad_down, other_up, other_down, sums, tiles, slots)
    sums = exchange(partial)
    result = pl.pallas_call(
        last_kernel,
        out_shape=shape(BAND, WIDE),
        in_specs=[smem(), smem(), *vmem(2)],
        out_specs=vmem(1)[0],
        scratch_shapes=[
            pltpu.VMEM((TILES, kept + 2 * GUARD, 128), F32),
            pltpu.VMEM((TILES, kept + 2 * GUARD, 128), F32),
            pltpu.VMEM((TILES, kept, 128), F32),
        ],
        compiler_params=params(),
        name="last",
    )(place, thresholds, trial, sums)
    blocks = lax.all_to_all(result.reshape(GROUP, SPLIT, WIDE), GROUP_AXES, split_axis=0, concat_axis=0, tiled=True)
    return pl.pallas_call(
        unpack_kernel,
        out_shape=shape(SPLIT, WIDE * GROUP),
        in_specs=vmem(1),
        out_specs=vmem(1)[0],
        compiler_params=params(),
        name="unpack",
    )(blocks)


def solution(mesh):
    fine = Mesh(mesh.devices.reshape(4, 4, 2, 2, 4), ALL_AXES)
    rows = P(ALL_AXES, None)
    in_specs = (rows, rows, rows, rows, P(ALL_AXES), P(), P())
    return jax.shard_map(body, mesh=fine, in_specs=in_specs, out_specs=rows, check_vma=False)
```

```python
import functools
import jax
import jax.numpy as jnp
from jax import lax
from jax.experimental import pallas as pl
from jax.experimental.pallas import tpu as pltpu
from jax.sharding import Mesh, PartitionSpec as P

TILE = 16
HALF = TILE // 2
LEVELS = 4
GROUP = 16
SPLIT = 8
BAND = GROUP * SPLIT
WIDE = 512
SIDE = 128
FRAME = WIDE + 2 * SIDE
DEEP = 80
NEAR = 40
MIDDLE = 32
REACH = 80
TILES = FRAME // 128
STRIP = 96
GUARD = 16
F32 = jnp.float32
BF16 = jnp.bfloat16

GROUP_AXES = ("zl", "core", "y")
BAND_AXES = ("x", "zh")
ALL_AXES = ("x", "zh", "zl", "core", "y")

G0, I0, H0, T0 = 0, FRAME, 2 * FRAME, 3 * FRAME
FACET = FRAME - 1
LANES = T0 + 128


def params():
    return pltpu.CompilerParams(vmem_limit_bytes=56 * 1024 * 1024)


def vmem(count):
    return [pl.BlockSpec(memory_space=pltpu.VMEM)] * count


def smem():
    return pl.BlockSpec(memory_space=pltpu.SMEM)


def pack_kernel(grad, image, weight, tile, facet, out):
    columns = grad.shape[1]
    for start, source in ((G0, grad), (I0, image), (H0, weight)):
        for block in range(GROUP):
            low, high = block * WIDE - SIDE, block * WIDE + WIDE + SIDE
            left, right = max(0, -low), max(0, high - columns)
            if left:
                out[block, :, start : start + left] = jnp.zeros((SPLIT, left), F32)
            if right:
                out[block, :, start + FRAME - right : start + FRAME] = jnp.zeros((SPLIT, right), F32)
            out[block, :, start + left : start + FRAME - right] = source[:, low + left : high - right]
    row, lane = iota((SPLIT, 128), 0), iota((SPLIT, 128), 1)
    ids = jnp.zeros((SPLIT, 128), jnp.int32)
    for index in range(SPLIT):
        ids = jnp.where(row == index, facet[index] + 1, ids)
    ids = ids.astype(F32)
    halves = jnp.concatenate(
        [tile[:, 0:128], tile[:, 128:256], jnp.zeros((SPLIT - 2, 128), F32)], axis=0
    )
    for block in range(GROUP):
        tail = out[block, :, I0 - 128 : I0]
        out[block, :, I0 - 128 : I0] = jnp.where(lane == 127, ids, tail)
        out[block, :, T0 : T0 + 128] = halves


def split(value):
    high = value.astype(BF16)
    low = (value - high.astype(F32)).astype(BF16)
    return high, low


def iota(shape, dim):
    return lax.broadcasted_iota(jnp.int32, shape, dim)


def dot(a, b):
    return jnp.dot(a, b, preferred_element_type=F32)


def taps_of(ids, tiles, slots, orders):
    rows = ids.shape[0]
    facet = jnp.broadcast_to(ids, (rows, 256))
    lane = iota((rows, 256), 1).astype(F32) + 1.0
    slot = jnp.sum(jnp.where(facet == lane, slots, 0.0), axis=1, keepdims=True)
    pick = (slot == lane).astype(F32).astype(BF16)
    row, col = iota((256, 256), 0), iota((256, 256), 1)
    parts = []
    for turned in orders:
        tap = 15 - col % 16 if turned else col % 16
        order = (row == tap * 16 + col // 16).astype(F32).astype(BF16)
        parts.append([dot(pick, dot(part, order).astype(BF16)) for part in split(tiles)])
    return parts


def table_of(tiles):
    return jnp.concatenate(
        [jnp.concatenate([tiles[g, half] for g in range(16)], axis=0) for half in range(2)], axis=1
    )


def turn(backward):
    kept = BAND + 2 * MIDDLE
    group = iota((kept, 256), 1) % 16
    value = backward[1 : 1 + kept]
    for step in range(1, TILE):
        value = jnp.where(group == step, backward[1 + step : 1 + step + kept], value)
    return value


def banded(taps, start, rows, offset, out):
    size = 16
    for part in range(rows // size):
        first = start + part * size
        place = iota((size, 256), 1) - iota((size, 256), 0) - (offset + part * size)
        bands = [(place >= p * REACH) & (place < p * REACH + TILE) for p in range(3)]
        skews = [
            pltpu.roll(taps[p, pl.ds(first, size), :], offset + part * size, 1, stride=1, stride_axis=0) for p in range(2)
        ]
        made = {}

        def rolled(which, turns):
            turns %= 16
            if (which, turns) not in made:
                made[which, turns] = pltpu.roll(skews[which], 16 * turns, 1) if turns else skews[which]
            return made[which, turns]

        for column in range(TILE):
            matrix = jnp.where(bands[2], rolled(1, 10 - column), 0.0)
            matrix = jnp.where(bands[1], rolled(0, 5 - column), matrix)
            matrix = jnp.where(bands[0], rolled(0, -column), matrix)
            out[column * rows + part * size : column * rows + (part + 1) * size, :] = matrix.astype(BF16)


def put_operand(value, pieces):
    rows = value.shape[0]
    high, low = split(value)
    for place, part in ((0, high), (REACH, low), (2 * REACH, high)):
        pieces[place : place + rows, :] = part
        if rows < REACH:
            pieces[place + rows : place + REACH, :] = jnp.zeros((REACH - rows, FRAME), BF16)
    pieces[3 * REACH : 256, :] = jnp.zeros((256 - 3 * REACH, FRAME), BF16)


def blur(matrix, rows, value, ahead, pieces, planes, emit):
    put_operand(value, pieces)
    planes[0 : TILE * rows, :] = dot(matrix[...], pieces[...])

    def total(at, first, count):
        if count == 1:
            return planes[first * rows + at : first * rows + at + 8, :]
        half = count // 2
        left = total(at, first, half)
        right = total(at, first + half, half)
        return left + pltpu.roll(right, FRAME - half if ahead else half, 1)

    for at in range(0, rows, 8):
        emit(at, pltpu.roll(total(at, 0, TILE), HALF if ahead else FRAME - HALF, 1))


def edges(band, block):
    return (block > 0).astype(F32), (block < GROUP - 1).astype(F32)


def row_inside(first, band):
    row = first + band * BAND
    return ((row >= 0) & (row < BAND * 16)).astype(F32)


def starlet(planes, total, spans, top, limits, band, sides):
    lane = iota((8, 128), 1)

    def level(depth):
        source, target = planes[depth % 2], planes[1 - depth % 2]
        d = 2**depth
        begin, end = spans[depth]

        def rows_from(start):
            inside = row_inside(top + start, band)
            edge, near, mid = 0.0625 * inside, 0.25 * inside, 0.375 * inside

            def at(t, offset):
                return source[t, pl.ds(start + GUARD + offset, 8), :]

            plain = [at(t, 0) for t in range(TILES)]
            down = [
                edge * (at(t, -2 * d) + at(t, 2 * d)) + near * (at(t, -d) + at(t, d)) + mid * plain[t]
                for t in range(TILES)
            ]

            def moved(s):
                right = [pltpu.roll(v, s, 1) for v in down]
                left = [pltpu.roll(v, 128 - s, 1) for v in down]
                return [
                    jnp.where(lane < s, right[max(t - 1, 0)], right[t])
                    + jnp.where(lane >= 128 - s, left[min(t + 1, TILES - 1)], left[t])
                    for t in range(TILES)
                ]

            outer, inner = moved(2 * d), moved(d)
            result = []
            for t in range(TILES):
                smoother = 0.0625 * outer[t] + 0.25 * inner[t] + 0.375 * down[t]
                if t == 0:
                    smoother = smoother * sides[0]
                if t == TILES - 1:
                    smoother = smoother * sides[1]
                detail = plain[t] - smoother
                if limits is None:
                    result.append((smoother, detail))
                    continue
                before = total[t, pl.ds(start, 8), :] if depth else plain[t]
                result.append((smoother, before - jnp.clip(detail, -limits[depth], limits[depth])))
            return result

        def chunk(index, carry):
            start = pl.multiple_of(begin + index * STRIP, 8)
            results = [(start + at, rows_from(start + at)) for at in range(0, STRIP, 8)]
            for first, result in results:
                for t in range(TILES):
                    if depth < LEVELS - 1:
                        target[t, pl.ds(first + GUARD, 8), :] = result[t][0]
                    if limits is not None:
                        total[t, pl.ds(first, 8), :] = result[t][1]
                    elif 0 < t < TILES - 1:
                        total[depth, pl.ds(first, 8), 128 * t - 128 : 128 * t] = result[t][1]
            return carry

        assert (end - begin) % STRIP == 0
        lax.fori_loop(0, (end - begin) // STRIP, chunk, 0)

    for depth in range(LEVELS):
        level(depth)


def clear_guards(plane, rows):
    plane[:, 0:GUARD, :] = jnp.zeros((TILES, GUARD, 128), F32)
    plane[:, GUARD + rows : 2 * GUARD + rows, :] = jnp.zeros((TILES, GUARD, 128), F32)


def put_partials(out, numerator, denominator):
    lane = iota((256, 128), 1)
    out[...] = jnp.where(lane == 0, numerator, jnp.where(lane == 1, denominator, 0.0))


def step_of(sums):
    total = jnp.sum(sums[...], axis=0, keepdims=True)
    lane = iota((1, 128), 1)
    return jnp.sum(jnp.where(lane == 0, total, 0.0)) / jnp.sum(jnp.where(lane == 1, total, 0.0))


def weigh_tile(matrix, values, weights, operand, pieces, planes, sums):
    carry = [sums[0], sums[1]]

    def weigh(at, blurred):
        value, heavy = values(at), weights(at)
        blurred = blurred[:, SIDE : SIDE + WIDE]
        carry[:] = carry[0] + value * value, carry[1] + heavy * blurred * blurred

    blur(matrix, 64, operand, True, pieces, planes, weigh)
    sums[0] = carry[0]
    sums[1] = carry[1]


def first_kernel(block, grad_up, grad_down, tiles, slots, partial, grad, matrix, pieces, planes, forward, sums):
    taps = taps_of(block[:, G0 + FACET : G0 + FRAME], table_of(tiles), slots[...].astype(F32) + 1.0, (False,))[0]
    for part in range(2):
        forward[part] = taps[part]
    grad[0:HALF, :] = grad_up[...]
    grad[HALF : HALF + BAND, :] = block[:, G0 : G0 + FRAME]
    grad[HALF + BAND : 2 * HALF + BAND, :] = grad_down[...]
    sums[...] = jnp.zeros((2, 8, WIDE), F32)

    def tile(index, carry):
        start = pl.multiple_of(index * 64, 64)
        banded(forward, start, 64, 0, matrix)
        weigh_tile(
            matrix,
            lambda at: block[pl.ds(start + at, 8), G0 + SIDE : G0 + SIDE + WIDE],
            lambda at: block[pl.ds(start + at, 8), H0 + SIDE : H0 + SIDE + WIDE],
            grad[pl.ds(start, REACH), :],
            pieces,
            planes,
            sums,
        )
        return carry

    lax.fori_loop(0, BAND // 64, tile, 0)
    put_partials(partial, jnp.sum(sums[0]), jnp.sum(sums[1]))


def matrices_kernel(above, own, below, tiles, slots, matrices, forward, adjoint):
    ids = jnp.concatenate([part[:, 127:128] for part in (above, own, below)], axis=0)
    ahead, back = taps_of(ids, table_of(tiles), slots[...].astype(F32) + 1.0, (False, True))
    for part in range(2):
        forward[part] = ahead[part]
        adjoint[part] = turn(back[part])

    def push_tile(index, carry):
        banded(forward, push_start(index), 64, 0, matrices.at[index])
        return carry

    def descend_tile(index, carry):
        banded(adjoint, pl.multiple_of(index * 64, 64), 64, 1, matrices.at[index + 4])
        return carry

    def last_tile(index, carry):
        banded(forward, pl.multiple_of(index * 64 + NEAR, 8), 64, 0, matrices.at[index + 7])
        return carry

    lax.fori_loop(0, 4, push_tile, 0)
    lax.fori_loop(0, 3, descend_tile, 0)
    lax.fori_loop(0, 2, last_tile, 0)


def push_start(index):
    return pl.multiple_of(jnp.minimum(index * 64, BAND + 2 * NEAR - 64), 16)


def middle_kernel(
    place, thresholds, block, grad_up, grad_down, other_up, other_down, totals, matrices,
    partial, trial,
    grad, image, weight, plane_a, plane_b, total, pieces, planes, pushed, sums,
):
    band, sides = place[0], edges(place[0], place[1])
    rows = BAND + 2 * DEEP
    near = BAND + 2 * NEAR
    kept = BAND + 2 * MIDDLE
    step = step_of(totals)
    for depth, start, lane, target, up, down in (
        (DEEP, 0, G0, grad, grad_up, grad_down),
        (DEEP, 0, I0, image, other_up, other_down),
        (NEAR, DEEP, H0, weight, other_up, other_down),
    ):
        target[0:depth, :] = up[start : start + depth, :]
        target[depth : depth + BAND, :] = block[:, lane : lane + FRAME]
        target[depth + BAND : 2 * depth + BAND, :] = down[start : start + depth, :]
    clear_guards(plane_a, rows)
    clear_guards(plane_b, rows)
    for t in range(TILES):
        lanes = slice(128 * t, 128 * t + 128)
        plane_a[t, GUARD : GUARD + rows, :] = image[:, lanes] - step * grad[:, lanes]
    limits = [step * thresholds[k] for k in range(LEVELS)]
    spans = ((0, 288),) * LEVELS
    starlet((plane_a, plane_b), total, spans, -DEEP, limits, band, sides)

    def change(first, count):
        new = jnp.concatenate([total[t, pl.ds(first, count), :] for t in range(TILES)], axis=1)
        return new - image[pl.ds(first, count), :]

    def push_tile(index, carry):
        start = push_start(index)

        def push(at, blurred):
            pushed[pl.ds(start + at, 8), :] = weight[pl.ds(start + at, 8), :] * blurred

        value = change(start + (DEEP - NEAR - HALF), REACH)
        blur(matrices.at[index], 64, value, True, pieces, planes, push)
        return carry

    lax.fori_loop(0, 4, push_tile, 0)

    def descend_tile(index, carry):
        start = pl.multiple_of(index * 64, 64)

        def descend(at, spread):
            inside = row_inside(start + (at - MIDDLE), band)
            value = (grad[pl.ds(start + (at + DEEP - MIDDLE), 8), :] + spread) * inside
            for t in range(TILES):
                lanes = slice(128 * t, 128 * t + 128)
                part = value[:, lanes]
                if t == 0:
                    part = part * sides[0]
                if t == TILES - 1:
                    part = part * sides[1]
                trial[1, pl.ds(start + at, 8), lanes] = part

        blur(matrices.at[index + 4], 64, pushed[pl.ds(start, REACH), :], False, pieces, planes, descend)
        return carry

    lax.fori_loop(0, kept // 64, descend_tile, 0)
    for t in range(TILES):
        trial[0, :, 128 * t : 128 * t + 128] = total[t, DEEP - MIDDLE : DEEP - MIDDLE + kept, :]

    sums[...] = jnp.zeros((2, 8, WIDE), F32)

    def last_tile(index, carry):
        start = pl.multiple_of(index * 64, 64)
        weigh_tile(
            matrices.at[index + 7],
            lambda at: trial[1, pl.ds(start + (at + MIDDLE), 8), SIDE : SIDE + WIDE],
            lambda at: weight[pl.ds(start + (at + NEAR), 8), SIDE : SIDE + WIDE],
            trial[1, pl.ds(start + (MIDDLE - HALF), REACH), :],
            pieces,
            planes,
            sums,
        )
        return carry

    lax.fori_loop(0, BAND // 64, last_tile, 0)
    put_partials(partial, jnp.sum(sums[0]), jnp.sum(sums[1]))


def details_kernel(place, trial, out, plane_a, plane_b, details):
    rows = BAND + 2 * MIDDLE
    clear_guards(plane_a, rows)
    clear_guards(plane_b, rows)

    def part(index, carry):
        for t in range(TILES):
            plane_a[t, GUARD : GUARD + rows, :] = trial[index, :, 128 * t : 128 * t + 128]
        starlet(
            (plane_a, plane_b), details, ((0, 192),) * LEVELS, -MIDDLE, None, place[0], edges(place[0], place[1])
        )
        for depth in range(LEVELS):
            out[index, depth] = details[depth, MIDDLE : MIDDLE + BAND, :]
        return carry

    lax.fori_loop(0, 2, part, 0)


def last_kernel(thresholds, trial, details, sums, out):
    step = step_of(sums)
    limits = [step * thresholds[k] for k in range(LEVELS)]

    def strip(index, carry):
        start = pl.multiple_of(index * 32, 32)
        rows = pl.ds(start, 32)
        wide = pl.ds(start + MIDDLE, 32)
        value = trial[0, wide, SIDE : SIDE + WIDE] - step * trial[1, wide, SIDE : SIDE + WIDE]
        for k in range(LEVELS):
            value = value - jnp.clip(details[0, k, rows, :] - step * details[1, k, rows, :], -limits[k], limits[k])
        out[rows, :] = value
        return carry

    lax.fori_loop(0, BAND // 32, strip, 0)


def unpack_kernel(blocks, out):
    for block in range(GROUP):
        out[:, block * WIDE : (block + 1) * WIDE] = blocks[block]


def shape(*sizes, dtype=F32):
    return jax.ShapeDtypeStruct(sizes, dtype)


def body(image_now, gradient, hessian_weight, psf_tiles, facet_of_row, tile_slot, thresholds):
    bands = 16
    band = lax.axis_index(BAND_AXES)
    place = jnp.stack([band, lax.axis_index(GROUP_AXES)]).astype(jnp.int32)
    sent = pl.pallas_call(
        pack_kernel,
        out_shape=shape(GROUP, SPLIT, LANES),
        in_specs=[*vmem(4), smem()],
        out_specs=vmem(1)[0],
        compiler_params=params(),
        name="pack",
    )(gradient, image_now, hessian_weight, psf_tiles, facet_of_row)
    block = lax.all_to_all(sent, GROUP_AXES, split_axis=0, concat_axis=0, tiled=True)
    block = block.reshape(BAND, LANES)
    down = [(i, i + 1) for i in range(bands - 1)]
    up = [(i + 1, i) for i in range(bands - 1)]

    grad_up = lax.ppermute(block[BAND - DEEP :, G0 : G0 + FRAME], BAND_AXES, down)
    grad_down = lax.ppermute(block[:DEEP, G0 : G0 + FRAME], BAND_AXES, up)
    later, grad_down = lax.optimization_barrier((block, grad_down))
    bottom = jnp.concatenate([later[BAND - DEEP :, I0:H0], later[BAND - NEAR :, H0:T0]])
    top = jnp.concatenate([later[:DEEP, I0:H0], later[:NEAR, H0:T0]])
    other_up = lax.ppermute(bottom, BAND_AXES, down)
    other_down = lax.ppermute(top, BAND_AXES, up)
    own = later[:, T0:].reshape(GROUP, SPLIT, 128)[:, 0:2].transpose(1, 0, 2)
    tiles = lax.all_to_all(
        jnp.broadcast_to(own[None], (bands, 2, GROUP, 128)), BAND_AXES, split_axis=0, concat_axis=0, tiled=True
    )
    near = BAND + 2 * NEAR
    kept = BAND + 2 * MIDDLE
    deep = BAND + 2 * DEEP
    slots = tile_slot.reshape(1, 256)
    partial = pl.pallas_call(
        first_kernel,
        grid=(1,),
        out_shape=shape(256, 128),
        in_specs=[
            *vmem(1),
            pl.BlockSpec((HALF, FRAME), lambda i: (DEEP // HALF - 1, 0)),
            pl.BlockSpec((HALF, FRAME), lambda i: (0, 0)),
            *vmem(2),
        ],
        out_specs=vmem(1)[0],
        scratch_shapes=[
            pltpu.VMEM((BAND + 2 * HALF, FRAME), F32),
            pltpu.VMEM((TILE * 64, 256), BF16),
            pltpu.VMEM((256, FRAME), BF16),
            pltpu.VMEM((TILE * 64, FRAME), F32),
            pltpu.VMEM((2, BAND, 256), F32),
            pltpu.VMEM((2, 8, WIDE), F32),
        ],
        compiler_params=params(),
        name="first",
    )(block, grad_up, grad_down, tiles, slots)

    def exchange(part):
        return lax.all_to_all(part, ALL_AXES, split_axis=0, concat_axis=0, tiled=True)

    partial, late_tiles = lax.optimization_barrier((partial, tiles))
    sums = exchange(partial)
    last = FRAME // 128 - 1
    matrices = pl.pallas_call(
        matrices_kernel,
        grid=(1,),
        out_shape=shape(9, TILE * 64, 256, dtype=BF16),
        in_specs=[
            pl.BlockSpec((NEAR, 128), lambda i: (DEEP // NEAR - 1, last)),
            pl.BlockSpec((BAND, 128), lambda i: (0, last)),
            pl.BlockSpec((NEAR, 128), lambda i: (0, last)),
            *vmem(2),
        ],
        out_specs=vmem(1)[0],
        scratch_shapes=[pltpu.VMEM((2, near, 256), F32), pltpu.VMEM((2, kept, 256), F32)],
        compiler_params=params(),
        cost_estimate=pl.CostEstimate(flops=10**9, bytes_accessed=6 * 10**6, transcendentals=0),
        name="matrices",
    )(grad_up, block, grad_down, late_tiles, slots)
    partial, trial = pl.pallas_call(
        middle_kernel,
        out_shape=(shape(256, 128), shape(2, kept, FRAME)),
        in_specs=[smem(), smem(), *vmem(7)],
        out_specs=vmem(2),
        scratch_shapes=[
            pltpu.VMEM((deep, FRAME), F32),
            pltpu.VMEM((deep, FRAME), F32),
            pltpu.VMEM((near, FRAME), F32),
            pltpu.VMEM((TILES, deep + 2 * GUARD, 128), F32),
            pltpu.VMEM((TILES, deep + 2 * GUARD, 128), F32),
            pltpu.VMEM((TILES, deep, 128), F32),
            pltpu.VMEM((256, FRAME), BF16),
            pltpu.VMEM((TILE * 64, FRAME), F32),
            pltpu.VMEM((near, FRAME), F32),
            pltpu.VMEM((2, 8, WIDE), F32),
        ],
        compiler_params=params(),
        name="middle",
    )(place, thresholds, block, grad_up, grad_down, other_up, other_down, sums, matrices)
    partial, late_trial = lax.optimization_barrier((partial, trial))
    sums = exchange(partial)
    details = pl.pallas_call(
        details_kernel,
        out_shape=shape(2, LEVELS, BAND, WIDE),
        in_specs=[smem(), *vmem(1)],
        out_specs=vmem(1)[0],
        scratch_shapes=[
            pltpu.VMEM((TILES, kept + 2 * GUARD, 128), F32),
            pltpu.VMEM((TILES, kept + 2 * GUARD, 128), F32),
            pltpu.VMEM((LEVELS, kept, WIDE), F32),
        ],
        compiler_params=params(),
        cost_estimate=pl.CostEstimate(flops=10**8, bytes_accessed=4 * 10**6, transcendentals=0),
        name="details",
    )(place, late_trial)
    result = pl.pallas_call(
        last_kernel,
        out_shape=shape(BAND, WIDE),
        in_specs=[smem(), *vmem(3)],
        out_specs=vmem(1)[0],
        compiler_params=params(),
        name="last",
    )(thresholds, late_trial, details, sums)
    blocks = lax.all_to_all(result.reshape(GROUP, SPLIT, WIDE), GROUP_AXES, split_axis=0, concat_axis=0, tiled=True)
    return pl.pallas_call(
        unpack_kernel,
        out_shape=shape(SPLIT, WIDE * GROUP),
        in_specs=vmem(1),
        out_specs=vmem(1)[0],
        compiler_params=params(),
        name="unpack",
    )(blocks)


def solution(mesh):
    fine = Mesh(mesh.devices.reshape(4, 4, 2, 2, 4), ALL_AXES)
    rows = P(ALL_AXES, None)
    in_specs = (rows, rows, rows, rows, P(ALL_AXES), P(), P())
    return jax.shard_map(body, mesh=fine, in_specs=in_specs, out_specs=rows, check_vma=False)
```

```python
import functools
import jax
import jax.numpy as jnp
from jax import lax
from jax.experimental import pallas as pl
from jax.experimental.pallas import tpu as pltpu
from jax.sharding import Mesh, PartitionSpec as P

TILE = 16
HALF = TILE // 2
LEVELS = 4
GROUP = 16
SPLIT = 8
BAND = GROUP * SPLIT
WIDE = 512
SIDE = 128
FRAME = WIDE + 2 * SIDE
DEEP = 80
NEAR = 40
MIDDLE = 32
REACH = 80
TILES = FRAME // 128
STRIP = 96
GUARD = 16
F32 = jnp.float32
BF16 = jnp.bfloat16

GROUP_AXES = ("zl", "core", "y")
BAND_AXES = ("x", "zh")
ALL_AXES = ("x", "zh", "zl", "core", "y")

G0, I0, H0, T0 = 0, FRAME, 2 * FRAME, 3 * FRAME
FACET = FRAME - 1
LANES = T0 + 128


def params():
    return pltpu.CompilerParams(vmem_limit_bytes=56 * 1024 * 1024)


def vmem(count):
    return [pl.BlockSpec(memory_space=pltpu.VMEM)] * count


def smem():
    return pl.BlockSpec(memory_space=pltpu.SMEM)


def pack_kernel(grad, image, weight, tile, facet, out):
    columns = grad.shape[1]
    for start, source in ((G0, grad), (I0, image), (H0, weight)):
        for block in range(GROUP):
            low, high = block * WIDE - SIDE, block * WIDE + WIDE + SIDE
            left, right = max(0, -low), max(0, high - columns)
            if left:
                out[block, :, start : start + left] = jnp.zeros((SPLIT, left), F32)
            if right:
                out[block, :, start + FRAME - right : start + FRAME] = jnp.zeros((SPLIT, right), F32)
            out[block, :, start + left : start + FRAME - right] = source[:, low + left : high - right]
    row, lane = iota((SPLIT, 128), 0), iota((SPLIT, 128), 1)
    ids = jnp.zeros((SPLIT, 128), jnp.int32)
    for index in range(SPLIT):
        ids = jnp.where(row == index, facet[index] + 1, ids)
    ids = ids.astype(F32)
    halves = jnp.concatenate(
        [tile[:, 0:128], tile[:, 128:256], jnp.zeros((SPLIT - 2, 128), F32)], axis=0
    )
    for block in range(GROUP):
        tail = out[block, :, I0 - 128 : I0]
        out[block, :, I0 - 128 : I0] = jnp.where(lane == 127, ids, tail)
        out[block, :, T0 : T0 + 128] = halves


def split(value):
    high = value.astype(BF16)
    low = (value - high.astype(F32)).astype(BF16)
    return high, low


def iota(shape, dim):
    return lax.broadcasted_iota(jnp.int32, shape, dim)


def dot(a, b):
    return jnp.dot(a, b, preferred_element_type=F32)


def taps_of(ids, tiles, slots, orders):
    rows = ids.shape[0]
    facet = jnp.broadcast_to(ids, (rows, 256))
    lane = iota((rows, 256), 1).astype(F32) + 1.0
    slot = jnp.sum(jnp.where(facet == lane, slots, 0.0), axis=1, keepdims=True)
    pick = (slot == lane).astype(F32).astype(BF16)
    row, col = iota((256, 256), 0), iota((256, 256), 1)
    parts = []
    for turned in orders:
        tap = 15 - col % 16 if turned else col % 16
        order = (row == tap * 16 + col // 16).astype(F32).astype(BF16)
        parts.append([dot(pick, dot(part, order).astype(BF16)) for part in split(tiles)])
    return parts


def table_of(tiles):
    return jnp.concatenate(
        [jnp.concatenate([tiles[g, half] for g in range(16)], axis=0) for half in range(2)], axis=1
    )


def turn(backward):
    kept = BAND + 2 * MIDDLE
    group = iota((kept, 256), 1) % 16
    value = backward[1 : 1 + kept]
    for step in range(1, TILE):
        value = jnp.where(group == step, backward[1 + step : 1 + step + kept], value)
    return value


def banded(taps, start, rows, offset, out):
    size = 16
    for part in range(rows // size):
        first = start + part * size
        place = iota((size, 256), 1) - iota((size, 256), 0) - (offset + part * size)
        bands = [(place >= p * REACH) & (place < p * REACH + TILE) for p in range(3)]
        skews = [
            pltpu.roll(taps[p, pl.ds(first, size), :], offset + part * size, 1, stride=1, stride_axis=0) for p in range(2)
        ]
        made = {}

        def rolled(which, turns):
            turns %= 16
            if (which, turns) not in made:
                made[which, turns] = pltpu.roll(skews[which], 16 * turns, 1) if turns else skews[which]
            return made[which, turns]

        for column in range(TILE):
            matrix = jnp.where(bands[2], rolled(1, 10 - column), 0.0)
            matrix = jnp.where(bands[1], rolled(0, 5 - column), matrix)
            matrix = jnp.where(bands[0], rolled(0, -column), matrix)
            out[column * rows + part * size : column * rows + (part + 1) * size, :] = matrix.astype(BF16)


def put_operand(value, pieces):
    rows = value.shape[0]
    high, low = split(value)
    for place, part in ((0, high), (REACH, low), (2 * REACH, high)):
        pieces[place : place + rows, :] = part
        if rows < REACH:
            pieces[place + rows : place + REACH, :] = jnp.zeros((REACH - rows, FRAME), BF16)
    pieces[3 * REACH : 256, :] = jnp.zeros((256 - 3 * REACH, FRAME), BF16)


def blur(matrix, rows, value, ahead, pieces, planes, emit):
    put_operand(value, pieces)
    planes[0 : TILE * rows, :] = dot(matrix[...], pieces[...])

    def total(at, first, count):
        if count == 1:
            return planes[first * rows + at : first * rows + at + 8, :]
        half = count // 2
        left = total(at, first, half)
        right = total(at, first + half, half)
        return left + pltpu.roll(right, FRAME - half if ahead else half, 1)

    for at in range(0, rows, 8):
        emit(at, pltpu.roll(total(at, 0, TILE), HALF if ahead else FRAME - HALF, 1))


def edges(band, block):
    return (block > 0).astype(F32), (block < GROUP - 1).astype(F32)


def row_inside(first, band):
    row = first + band * BAND
    return ((row >= 0) & (row < BAND * 16)).astype(F32)


def starlet(planes, total, spans, top, limits, band, sides):
    lane = iota((8, 128), 1)

    def level(depth):
        source, target = planes[depth % 2], planes[1 - depth % 2]
        d = 2**depth
        begin, end = spans[depth]

        def rows_from(start):
            inside = row_inside(top + start, band)
            edge, near, mid = 0.0625 * inside, 0.25 * inside, 0.375 * inside

            def at(t, offset):
                return source[t, pl.ds(start + GUARD + offset, 8), :]

            plain = [at(t, 0) for t in range(TILES)]
            down = [
                edge * (at(t, -2 * d) + at(t, 2 * d)) + near * (at(t, -d) + at(t, d)) + mid * plain[t]
                for t in range(TILES)
            ]

            def moved(s):
                right = [pltpu.roll(v, s, 1) for v in down]
                left = [pltpu.roll(v, 128 - s, 1) for v in down]
                return [
                    jnp.where(lane < s, right[max(t - 1, 0)], right[t])
                    + jnp.where(lane >= 128 - s, left[min(t + 1, TILES - 1)], left[t])
                    for t in range(TILES)
                ]

            outer, inner = moved(2 * d), moved(d)
            result = []
            for t in range(TILES):
                smoother = 0.0625 * outer[t] + 0.25 * inner[t] + 0.375 * down[t]
                if t == 0:
                    smoother = smoother * sides[0]
                if t == TILES - 1:
                    smoother = smoother * sides[1]
                detail = plain[t] - smoother
                if limits is None:
                    result.append((smoother, detail))
                    continue
                before = total[t, pl.ds(start, 8), :] if depth else plain[t]
                result.append((smoother, before - jnp.clip(detail, -limits[depth], limits[depth])))
            return result

        def chunk(index, carry):
            start = pl.multiple_of(begin + index * STRIP, 8)
            results = [(start + at, rows_from(start + at)) for at in range(0, STRIP, 8)]
            for first, result in results:
                for t in range(TILES):
                    if depth < LEVELS - 1:
                        target[t, pl.ds(first + GUARD, 8), :] = result[t][0]
                    if limits is not None:
                        total[t, pl.ds(first, 8), :] = result[t][1]
                    elif 0 < t < TILES - 1:
                        total[depth, pl.ds(first, 8), 128 * t - 128 : 128 * t] = result[t][1]
            return carry

        assert (end - begin) % STRIP == 0
        lax.fori_loop(0, (end - begin) // STRIP, chunk, 0)

    for depth in range(LEVELS):
        level(depth)


def clear_guards(plane, rows):
    plane[:, 0:GUARD, :] = jnp.zeros((TILES, GUARD, 128), F32)
    plane[:, GUARD + rows : 2 * GUARD + rows, :] = jnp.zeros((TILES, GUARD, 128), F32)


def put_partials(out, numerator, denominator):
    lane = iota((256, 128), 1)
    out[...] = jnp.where(lane == 0, numerator, jnp.where(lane == 1, denominator, 0.0))


def step_of(sums):
    total = jnp.sum(sums[...], axis=0, keepdims=True)
    lane = iota((1, 128), 1)
    return jnp.sum(jnp.where(lane == 0, total, 0.0)) / jnp.sum(jnp.where(lane == 1, total, 0.0))


def weigh_tile(matrix, values, weights, operand, pieces, planes, sums):
    carry = [sums[0], sums[1]]

    def weigh(at, blurred):
        value, heavy = values(at), weights(at)
        blurred = blurred[:, SIDE : SIDE + WIDE]
        carry[:] = carry[0] + value * value, carry[1] + heavy * blurred * blurred

    blur(matrix, 64, operand, True, pieces, planes, weigh)
    sums[0] = carry[0]
    sums[1] = carry[1]


def first_kernel(block, grad_up, grad_down, tiles, slots, partial, grad, matrix, pieces, planes, forward, sums):
    taps = taps_of(block[:, G0 + FACET : G0 + FRAME], table_of(tiles), slots[...].astype(F32) + 1.0, (False,))[0]
    for part in range(2):
        forward[part] = taps[part]
    grad[0:HALF, :] = grad_up[...]
    grad[HALF : HALF + BAND, :] = block[:, G0 : G0 + FRAME]
    grad[HALF + BAND : 2 * HALF + BAND, :] = grad_down[...]
    sums[...] = jnp.zeros((2, 8, WIDE), F32)

    def tile(index, carry):
        start = pl.multiple_of(index * 64, 64)
        banded(forward, start, 64, 0, matrix)
        weigh_tile(
            matrix,
            lambda at: block[pl.ds(start + at, 8), G0 + SIDE : G0 + SIDE + WIDE],
            lambda at: block[pl.ds(start + at, 8), H0 + SIDE : H0 + SIDE + WIDE],
            grad[pl.ds(start, REACH), :],
            pieces,
            planes,
            sums,
        )
        return carry

    lax.fori_loop(0, BAND // 64, tile, 0)
    put_partials(partial, jnp.sum(sums[0]), jnp.sum(sums[1]))


def matrices_kernel(above, own, below, tiles, slots, matrices, forward, adjoint):
    ids = jnp.concatenate([part[:, 127:128] for part in (above, own, below)], axis=0)
    ahead, back = taps_of(ids, table_of(tiles), slots[...].astype(F32) + 1.0, (False, True))
    for part in range(2):
        forward[part] = ahead[part]
        adjoint[part] = turn(back[part])

    def push_tile(index, carry):
        banded(forward, push_start(index), 64, 0, matrices.at[index])
        return carry

    def descend_tile(index, carry):
        banded(adjoint, pl.multiple_of(index * 64, 64), 64, 1, matrices.at[index + 4])
        return carry

    def last_tile(index, carry):
        banded(forward, pl.multiple_of(index * 64 + NEAR, 8), 64, 0, matrices.at[index + 7])
        return carry

    lax.fori_loop(0, 4, push_tile, 0)
    lax.fori_loop(0, 3, descend_tile, 0)
    lax.fori_loop(0, 2, last_tile, 0)


def push_start(index):
    return pl.multiple_of(jnp.minimum(index * 64, BAND + 2 * NEAR - 64), 16)


def middle_kernel(
    place, thresholds, block, grad_up, grad_down, other_up, other_down, totals, stored,
    partial, trial,
    grad, image, weight, plane_a, plane_b, total, pieces, planes, pushed, sums, matrices, arrived,
):
    fetch = pltpu.make_async_copy(stored, matrices, arrived)
    fetch.start()
    band, sides = place[0], edges(place[0], place[1])
    rows = BAND + 2 * DEEP
    near = BAND + 2 * NEAR
    kept = BAND + 2 * MIDDLE
    step = step_of(totals)
    for depth, start, lane, target, up, down in (
        (DEEP, 0, G0, grad, grad_up, grad_down),
        (DEEP, 0, I0, image, other_up, other_down),
        (NEAR, DEEP, H0, weight, other_up, other_down),
    ):
        target[0:depth, :] = up[start : start + depth, :]
        target[depth : depth + BAND, :] = block[:, lane : lane + FRAME]
        target[depth + BAND : 2 * depth + BAND, :] = down[start : start + depth, :]
    clear_guards(plane_a, rows)
    clear_guards(plane_b, rows)
    for t in range(TILES):
        lanes = slice(128 * t, 128 * t + 128)
        plane_a[t, GUARD : GUARD + rows, :] = image[:, lanes] - step * grad[:, lanes]
    limits = [step * thresholds[k] for k in range(LEVELS)]
    spans = ((0, 288),) * LEVELS
    starlet((plane_a, plane_b), total, spans, -DEEP, limits, band, sides)

    def change(first, count):
        new = jnp.concatenate([total[t, pl.ds(first, count), :] for t in range(TILES)], axis=1)
        return new - image[pl.ds(first, count), :]

    def push_tile(index, carry):
        start = push_start(index)

        def push(at, blurred):
            pushed[pl.ds(start + at, 8), :] = weight[pl.ds(start + at, 8), :] * blurred

        value = change(start + (DEEP - NEAR - HALF), REACH)
        blur(matrices.at[index], 64, value, True, pieces, planes, push)
        return carry

    fetch.wait()
    lax.fori_loop(0, 4, push_tile, 0)

    def descend_tile(index, carry):
        start = pl.multiple_of(index * 64, 64)

        def descend(at, spread):
            inside = row_inside(start + (at - MIDDLE), band)
            value = (grad[pl.ds(start + (at + DEEP - MIDDLE), 8), :] + spread) * inside
            for t in range(TILES):
                lanes = slice(128 * t, 128 * t + 128)
                part = value[:, lanes]
                if t == 0:
                    part = part * sides[0]
                if t == TILES - 1:
                    part = part * sides[1]
                trial[1, pl.ds(start + at, 8), lanes] = part

        blur(matrices.at[index + 4], 64, pushed[pl.ds(start, REACH), :], False, pieces, planes, descend)
        return carry

    lax.fori_loop(0, kept // 64, descend_tile, 0)
    for t in range(TILES):
        trial[0, :, 128 * t : 128 * t + 128] = total[t, DEEP - MIDDLE : DEEP - MIDDLE + kept, :]

    sums[...] = jnp.zeros((2, 8, WIDE), F32)

    def last_tile(index, carry):
        start = pl.multiple_of(index * 64, 64)
        weigh_tile(
            matrices.at[index + 7],
            lambda at: trial[1, pl.ds(start + (at + MIDDLE), 8), SIDE : SIDE + WIDE],
            lambda at: weight[pl.ds(start + (at + NEAR), 8), SIDE : SIDE + WIDE],
            trial[1, pl.ds(start + (MIDDLE - HALF), REACH), :],
            pieces,
            planes,
            sums,
        )
        return carry

    lax.fori_loop(0, BAND // 64, last_tile, 0)
    put_partials(partial, jnp.sum(sums[0]), jnp.sum(sums[1]))


def details_kernel(place, trial, out, plane_a, plane_b, details):
    rows = BAND + 2 * MIDDLE
    clear_guards(plane_a, rows)
    clear_guards(plane_b, rows)

    def part(index, carry):
        for t in range(TILES):
            plane_a[t, GUARD : GUARD + rows, :] = trial[index, :, 128 * t : 128 * t + 128]
        starlet(
            (plane_a, plane_b), details, ((0, 192),) * LEVELS, -MIDDLE, None, place[0], edges(place[0], place[1])
        )
        for depth in range(LEVELS):
            out[index, depth] = details[depth, MIDDLE : MIDDLE + BAND, :]
        return carry

    lax.fori_loop(0, 2, part, 0)


def last_kernel(thresholds, trial, details, sums, out):
    step = step_of(sums)
    limits = [step * thresholds[k] for k in range(LEVELS)]

    def strip(index, carry):
        start = pl.multiple_of(index * 32, 32)
        rows = pl.ds(start, 32)
        wide = pl.ds(start + MIDDLE, 32)
        value = trial[0, wide, SIDE : SIDE + WIDE] - step * trial[1, wide, SIDE : SIDE + WIDE]
        for k in range(LEVELS):
            value = value - jnp.clip(details[0, k, rows, :] - step * details[1, k, rows, :], -limits[k], limits[k])
        out[rows, :] = value
        return carry

    lax.fori_loop(0, BAND // 32, strip, 0)


def unpack_kernel(blocks, out):
    for block in range(GROUP):
        out[:, block * WIDE : (block + 1) * WIDE] = blocks[block]


def shape(*sizes, dtype=F32):
    return jax.ShapeDtypeStruct(sizes, dtype)


def body(image_now, gradient, hessian_weight, psf_tiles, facet_of_row, tile_slot, thresholds):
    bands = 16
    band = lax.axis_index(BAND_AXES)
    place = jnp.stack([band, lax.axis_index(GROUP_AXES)]).astype(jnp.int32)
    sent = pl.pallas_call(
        pack_kernel,
        out_shape=shape(GROUP, SPLIT, LANES),
        in_specs=[*vmem(4), smem()],
        out_specs=vmem(1)[0],
        compiler_params=params(),
        name="pack",
    )(gradient, image_now, hessian_weight, psf_tiles, facet_of_row)
    block = lax.all_to_all(sent, GROUP_AXES, split_axis=0, concat_axis=0, tiled=True)
    block = block.reshape(BAND, LANES)
    down = [(i, i + 1) for i in range(bands - 1)]
    up = [(i + 1, i) for i in range(bands - 1)]

    grad_up = lax.ppermute(block[BAND - DEEP :, G0 : G0 + FRAME], BAND_AXES, down)
    grad_down = lax.ppermute(block[:DEEP, G0 : G0 + FRAME], BAND_AXES, up)
    later, grad_down = lax.optimization_barrier((block, grad_down))
    bottom = jnp.concatenate([later[BAND - DEEP :, I0:H0], later[BAND - NEAR :, H0:T0]])
    top = jnp.concatenate([later[:DEEP, I0:H0], later[:NEAR, H0:T0]])
    other_up = lax.ppermute(bottom, BAND_AXES, down)
    other_down = lax.ppermute(top, BAND_AXES, up)
    own = later[:, T0:].reshape(GROUP, SPLIT, 128)[:, 0:2].transpose(1, 0, 2)
    tiles = lax.all_to_all(
        jnp.broadcast_to(own[None], (bands, 2, GROUP, 128)), BAND_AXES, split_axis=0, concat_axis=0, tiled=True
    )
    near = BAND + 2 * NEAR
    kept = BAND + 2 * MIDDLE
    deep = BAND + 2 * DEEP
    slots = tile_slot.reshape(1, 256)
    partial = pl.pallas_call(
        first_kernel,
        grid=(1,),
        out_shape=shape(256, 128),
        in_specs=[
            *vmem(1),
            pl.BlockSpec((HALF, FRAME), lambda i: (DEEP // HALF - 1, 0)),
            pl.BlockSpec((HALF, FRAME), lambda i: (0, 0)),
            *vmem(2),
        ],
        out_specs=vmem(1)[0],
        scratch_shapes=[
            pltpu.VMEM((BAND + 2 * HALF, FRAME), F32),
            pltpu.VMEM((TILE * 64, 256), BF16),
            pltpu.VMEM((256, FRAME), BF16),
            pltpu.VMEM((TILE * 64, FRAME), F32),
            pltpu.VMEM((2, BAND, 256), F32),
            pltpu.VMEM((2, 8, WIDE), F32),
        ],
        compiler_params=params(),
        name="first",
    )(block, grad_up, grad_down, tiles, slots)

    def exchange(part):
        return lax.all_to_all(part, ALL_AXES, split_axis=0, concat_axis=0, tiled=True)

    partial, late_tiles = lax.optimization_barrier((partial, tiles))
    sums = exchange(partial)
    last = FRAME // 128 - 1
    matrices = pl.pallas_call(
        matrices_kernel,
        grid=(1,),
        out_shape=shape(9, TILE * 64, 256, dtype=BF16),
        in_specs=[
            pl.BlockSpec((NEAR, 128), lambda i: (DEEP // NEAR - 1, last)),
            pl.BlockSpec((BAND, 128), lambda i: (0, last)),
            pl.BlockSpec((NEAR, 128), lambda i: (0, last)),
            *vmem(2),
        ],
        out_specs=vmem(1)[0],
        scratch_shapes=[pltpu.VMEM((2, near, 256), F32), pltpu.VMEM((2, kept, 256), F32)],
        compiler_params=params(),
        cost_estimate=pl.CostEstimate(flops=10**9, bytes_accessed=6 * 10**6, transcendentals=0),
        name="matrices",
    )(grad_up, block, grad_down, late_tiles, slots)
    partial, trial = pl.pallas_call(
        middle_kernel,
        out_shape=(shape(256, 128), shape(2, kept, FRAME)),
        in_specs=[smem(), smem(), *vmem(6), pl.BlockSpec(memory_space=pl.ANY)],
        out_specs=vmem(2),
        scratch_shapes=[
            pltpu.VMEM((deep, FRAME), F32),
            pltpu.VMEM((deep, FRAME), F32),
            pltpu.VMEM((near, FRAME), F32),
            pltpu.VMEM((TILES, deep + 2 * GUARD, 128), F32),
            pltpu.VMEM((TILES, deep + 2 * GUARD, 128), F32),
            pltpu.VMEM((TILES, deep, 128), F32),
            pltpu.VMEM((256, FRAME), BF16),
            pltpu.VMEM((TILE * 64, FRAME), F32),
            pltpu.VMEM((near, FRAME), F32),
            pltpu.VMEM((2, 8, WIDE), F32),
            pltpu.VMEM((9, TILE * 64, 256), BF16),
            pltpu.SemaphoreType.DMA,
        ],
        compiler_params=params(),
        name="middle",
    )(place, thresholds, block, grad_up, grad_down, other_up, other_down, sums, matrices)
    partial, late_trial = lax.optimization_barrier((partial, trial))
    sums = exchange(partial)
    details = pl.pallas_call(
        details_kernel,
        out_shape=shape(2, LEVELS, BAND, WIDE),
        in_specs=[smem(), *vmem(1)],
        out_specs=vmem(1)[0],
        scratch_shapes=[
            pltpu.VMEM((TILES, kept + 2 * GUARD, 128), F32),
            pltpu.VMEM((TILES, kept + 2 * GUARD, 128), F32),
            pltpu.VMEM((LEVELS, kept, WIDE), F32),
        ],
        compiler_params=params(),
        cost_estimate=pl.CostEstimate(flops=10**8, bytes_accessed=4 * 10**6, transcendentals=0),
        name="details",
    )(place, late_trial)
    result = pl.pallas_call(
        last_kernel,
        out_shape=shape(BAND, WIDE),
        in_specs=[smem(), *vmem(3)],
        out_specs=vmem(1)[0],
        compiler_params=params(),
        name="last",
    )(thresholds, late_trial, details, sums)
    blocks = lax.all_to_all(result.reshape(GROUP, SPLIT, WIDE), GROUP_AXES, split_axis=0, concat_axis=0, tiled=True)
    return pl.pallas_call(
        unpack_kernel,
        out_shape=shape(SPLIT, WIDE * GROUP),
        in_specs=vmem(1),
        out_specs=vmem(1)[0],
        compiler_params=params(),
        name="unpack",
    )(blocks)


def solution(mesh):
    fine = Mesh(mesh.devices.reshape(4, 4, 2, 2, 4), ALL_AXES)
    rows = P(ALL_AXES, None)
    in_specs = (rows, rows, rows, rows, P(ALL_AXES), P(), P())
    return jax.shard_map(body, mesh=fine, in_specs=in_specs, out_specs=rows, check_vma=False)
```
